256 devices in a mesh: lon: 32 (over x_lo, z, core), lat: 8 (over y, x_hi).
Axes of the slice: x: 4 (x_hi: 2, x_lo: 2; x = x_hi * 2 + x_lo), y: 4, z: 8, core: 2. Of those that a mesh axis runs over, the one named last changes fastest.
Arguments:
- tokens: bfloat16 [240, 384, 512], P('lat', 'lon'), may hold values from -50 to 50
- gain_one: float32 [512], replicated, may hold values from 0.1 to 1.9
- w_qkv_one: bfloat16 [512, 1536], replicated, may hold values from -2.1213203 to 2.1213203
- w_out_one: bfloat16 [512, 512], replicated, may hold values from -0.25 to 0.25
- gain_two: float32 [512], replicated, may hold values from 0.1 to 1.9
- w_qkv_two: bfloat16 [512, 1536], replicated, may hold values from -2.1213203 to 2.1213203
- w_out_two: bfloat16 [512, 512], replicated, may hold values from -0.25 to 0.25
- merge_gain: float32 [2048], replicated, may hold values from 0.1 to 1.9
- w_merge: bfloat16 [2048, 1024], replicated, may hold values from -0.125 to 0.125
Outputs:
- merged: bfloat16 [8, 15, 192, 1024], P('lat', None, None, 'lon')
The draws below stay inside these ranges and needn't reach their ends.
All inputs are finite; a program needn't handle non-finite values.
Results may differ from the reference program's by a relative error of at most 0.02.
The reference program's roundings to bfloat16 on the way count: a program that leaves them out, or rounds other values in their place, can miss the bound.
Values may be sent and summed in bfloat16 or wider, within the bound.
A program may use at most 64 MiB of HBM per device.

```python
import math
import jax
import jax.numpy as jnp
from jax import lax

D = 512
HEADS = 8
HEAD_DIM = 64
WH = 6
WW = 12
LAT_DEV = 30
SH = 3
SW = 6
LATS = 240
LONS = 384
N_LAT = 8


def projection(key, spot, low, high):
    key = jax.random.fold_in(key, spot)
    first, second = jax.random.split(key)
    base = jnp.clip(jax.random.normal(first, (D, 3 * D), jnp.float32), -4.0, 4.0) * D ** (-0.5)
    heads = jnp.exp(jax.random.uniform(second, (HEADS,), jnp.float32, math.log(low), math.log(high)))
    per_col = jnp.repeat(heads, HEAD_DIM)
    scale = jnp.concatenate([per_col, per_col, jnp.ones((D,), jnp.float32)])
    return (base * scale[None, :]).astype(jnp.bfloat16)


def draw_w_qkv_one(key, part):
    return projection(key, 21, 1.0, 1.0)


def draw_w_qkv_two(key, part):
    return projection(key, 37, 1.0, 1.0)


def draw_tokens(key, part):
    key = jax.random.fold_in(key, 5)
    first, second, third = jax.random.split(key, 3)
    rows = jnp.exp(jax.random.uniform(second, (LATS, LONS, 1), jnp.float32, math.log(0.3), math.log(3.0)))
    cols = jnp.exp(jax.random.uniform(third, (D,), jnp.float32, math.log(0.3), math.log(3.0)))
    base = jnp.clip(jax.random.normal(first, (LATS, LONS, D), jnp.float32), -4.0, 4.0)
    return (base * rows * cols).astype(jnp.bfloat16)


def normal_values(key, extent, scale, bound, kind=jnp.bfloat16):
    drawn = scale * jax.random.normal(key, extent, jnp.float32)
    return jnp.clip(drawn, min=-bound, max=bound).astype(kind)


def setup_inputs(seed: int = 0) -> dict:
    key_of = jax.random.split(jax.random.key(seed), 10)
    return {
        "tokens": draw_tokens(jax.random.fold_in(key_of[9], 71), 0),
        "gain_one": jnp.clip(1.0 + 0.18 * jax.random.normal(key_of[1], (D,), jnp.float32), 0.1, 1.9),
        "w_qkv_one": draw_w_qkv_one(jax.random.fold_in(key_of[9], 71), 0),
        "w_out_one": normal_values(key_of[3], (D, D), D ** -0.5, 0.25),
        "gain_two": jnp.clip(1.0 + 0.18 * jax.random.normal(key_of[4], (D,), jnp.float32), 0.1, 1.9),
        "w_qkv_two": draw_w_qkv_two(jax.random.fold_in(key_of[9], 71), 0),
        "w_out_two": normal_values(key_of[6], (D, D), D ** -0.5, 0.25),
        "merge_gain": jnp.clip(1.0 + 0.18 * jax.random.normal(key_of[7], (4 * D,), jnp.float32), 0.1, 1.9),
        "w_merge": normal_values(key_of[8], (4 * D, 2 * D), (4 * D) ** -0.5, 0.125),
    }


def layer_norm(values, gain):
    center = lax.optimization_barrier(jnp.mean(values, axis=-1, keepdims=True))
    spread = lax.optimization_barrier(jnp.mean(jnp.square(values - center), axis=-1, keepdims=True))
    return ((values - center) * lax.rsqrt(spread + 1e-05) * gain).astype(jnp.bfloat16)

def attend(window_set, gain, w_qkv, w_out, allowed):
    count, length, width = window_set.shape
    values = window_set.astype(jnp.float32)
    normed = layer_norm(values, gain.astype(jnp.float32))
    packed = jnp.dot(normed.reshape(count * length, width), w_qkv, preferred_element_type=jnp.float32).astype(jnp.bfloat16)
    packed = packed.reshape(count, length, 3, HEADS, HEAD_DIM)
    query = packed[:, :, 0].astype(jnp.float32)
    keys = packed[:, :, 1].astype(jnp.float32)
    vals = packed[:, :, 2].astype(jnp.float32)
    scores = jnp.einsum('bqhd,bkhd->bhqk', query, keys) * HEAD_DIM ** (-0.5)
    scores = jnp.where(allowed, scores, -jnp.inf)
    top = lax.optimization_barrier(jnp.max(scores, axis=-1, keepdims=True))
    expo = jnp.exp(scores - top)
    probs = (expo / lax.optimization_barrier(jnp.sum(expo, axis=-1, keepdims=True))).astype(jnp.bfloat16)
    mixed = jnp.einsum('bhqk,bkhd->bqhd', probs.astype(jnp.float32), vals).astype(jnp.bfloat16)
    update = jnp.dot(mixed.reshape(count * length, width), w_out, preferred_element_type=jnp.float32)
    return (values + update.reshape(count, length, width)).astype(jnp.bfloat16)

def run_block(field, gain, w_qkv, w_out, masked):
    lats, lons, width = field.shape
    rows_w = lats // WH
    cols_w = lons // WW
    grid = field.reshape(rows_w, WH, cols_w, WW, width).transpose(0, 2, 1, 3, 4).reshape(rows_w, cols_w, WH * WW, width)
    token = jnp.arange(WH * WW)
    group = token // WW >= SH
    same = group[:, None] == group[None, :]

    def one_row(item):
        row, index = item
        if masked:
            allowed = same | (index != rows_w - 1)
        else:
            allowed = True
        return attend(row, gain, w_qkv, w_out, allowed)
    result = lax.map(one_row, (grid, jnp.arange(rows_w, dtype=jnp.int32)))
    return result.reshape(rows_w, cols_w, WH, WW, width).transpose(0, 2, 1, 3, 4).reshape(lats, lons, width)

def merge_patches(field, gain, w_merge):
    rows, cols, width = field.shape
    quads = field.reshape(rows // 2, 2, cols // 2, 2, width).transpose(0, 2, 3, 1, 4).reshape(rows // 2, cols // 2, 4 * width)
    normed = layer_norm(quads.astype(jnp.float32), gain.astype(jnp.float32))
    result = jnp.dot(normed.reshape(rows // 2 * (cols // 2), 4 * width), w_merge, preferred_element_type=jnp.float32)
    return result.astype(jnp.bfloat16).reshape(rows // 2, cols // 2, 2 * width)

def reference(tokens, gain_one, w_qkv_one, w_out_one, gain_two, w_qkv_two, w_out_two, merge_gain, w_merge):
    block_one = run_block(tokens, gain_one, w_qkv_one, w_out_one, False)
    shifted = jnp.roll(block_one, (-SH, -SW), axis=(0, 1))
    block_two_shifted = run_block(shifted, gain_two, w_qkv_two, w_out_two, True)
    block_two = jnp.roll(block_two_shifted, (SH, SW), axis=(0, 1))
    bands = block_two.reshape(N_LAT, LAT_DEV, LONS, D)
    return lax.map(lambda band: merge_patches(band, merge_gain, w_merge), bands)
```

```python
import functools

import jax
import jax.numpy as jnp
import numpy as np
from jax import lax
from jax.experimental import pallas as pl
from jax.experimental.pallas import tpu as pltpu
from jax.sharding import PartitionSpec as P

MESH = pl.DeviceIdType.MESH
BF = jnp.bfloat16
F32 = jnp.float32

D = 512
SLOTS = 80
WINDOWS = 5
WEST = 48
FEATS = 32


def tables(n_lon):
    first = np.zeros((WINDOWS * SLOTS, 12 * 32), np.float32)
    for w in range(WINDOWS):
        for r in range(6):
            for c in range(12):
                if c < 6:
                    slot = (0 if r < 3 else 18) + (r % 3) * 6 + c
                else:
                    slot = (54 if r < 3 else 36) + (r % 3) * 6 + c - 6
                first[w * SLOTS + slot, c * 32 + 6 * w + r] = 1
    second = np.zeros((SLOTS, 2 * SLOTS + 2 * WEST), np.float32)
    for r in range(6):
        for c in range(12):
            within = (r % 3) * 6 + c % 6
            if c < 6:
                source = 36 + within if r < 3 else SLOTS + 54 + within
            else:
                source = 2 * SLOTS + (18 + within if r < 3 else WEST + within)
            second[r * 12 + c, source] = 1
    high = np.zeros((256, 3 * SLOTS), np.float32)
    north = np.zeros((256, WEST), np.float32)
    low = np.zeros((256, 3 * SLOTS), np.float32)
    for corner in range(4):
        for i in range(15):
            for j in range(6):
                row = 2 * i + corner % 2
                col = 2 * j + corner // 2
                spot = corner * 64 + (i % 8) * 8 + j
                if row < 3:
                    north[spot, 4 + row * 12 + col] = 1
                    continue
                w, r = divmod(row - 3, 6)
                if i >= 8:
                    high[spot, (w - 2) * SLOTS + r * 12 + col] = 1
                else:
                    low[spot, w * SLOTS + r * 12 + col] = 1
    circle = np.zeros((n_lon * 16, 512), np.float32)
    for s in range(n_lon):
        for half in range(2):
            for j in range(6):
                circle[s * 16 + half * 8 + j, half * 256 + (6 * s + 3 + j) % (6 * n_lon)] = 1
    return [jnp.asarray(t, BF) for t in (first, second, high, north, low, circle)]


def dot(a, b):
    return jnp.dot(a, b, preferred_element_type=F32)


def layer_norm(x, gain):
    center = jnp.mean(x, axis=-1, keepdims=True)
    d = x - center
    spread = jnp.mean(d * d, axis=-1, keepdims=True)
    return (d * lax.rsqrt(spread + 1e-05) * gain).astype(BF)


def by_head(block):
    lane = lax.broadcasted_iota(jnp.int32, block.shape, 1) // 64
    empty = jnp.zeros((128 - SLOTS, 256), BF)
    parts = []
    for h in range(4):
        parts += [jnp.where(lane == h, block, jnp.zeros_like(block)), empty]
    return jnp.concatenate(parts, axis=0)


def attend(qkv, base, allowed):
    mixed = []
    for g in range(2):
        rows = pl.ds(base, SLOTS)
        q = qkv[rows, g * 256 : g * 256 + 256]
        k = by_head(qkv[rows, D + g * 256 : D + g * 256 + 256])
        v = by_head(qkv[rows, 2 * D + g * 256 : 2 * D + g * 256 + 256])
        scores = lax.dot_general(q, k, (((1,), (1,)), ((), ())), preferred_element_type=F32)
        probs = []
        for h in range(4):
            s = jnp.where(allowed, scores[:, h * 128 : h * 128 + 128], -1e30)
            top = jnp.max(s, axis=-1, keepdims=True)
            expo = jnp.exp((s - top) * 0.125)
            total = jnp.sum(expo, axis=-1, keepdims=True)
            probs.append((expo * (1.0 / total)).astype(BF))
        mixed.append(dot(jnp.concatenate(probs, axis=1), v).astype(BF))
    return jnp.concatenate(mixed, axis=1)


def spread_out(result, slabs, chunk):
    parts = result.reshape(2, 4, 8, 1024)
    lane = lax.broadcasted_iota(jnp.int32, (16, 128), 1)
    left = lane < 64
    even = (lane // 32) % 2 == 0
    for t in range(8):
        a = [parts[:, v, :, t * 128 : t * 128 + 128].reshape(16, 128) for v in range(4)]
        b0 = jnp.where(left, a[0], pltpu.roll(a[2], 64, 1))
        b1 = jnp.where(left, a[1], pltpu.roll(a[3], 64, 1))
        b2 = jnp.where(left, pltpu.roll(a[0], 64, 1), a[2])
        b3 = jnp.where(left, pltpu.roll(a[1], 64, 1), a[3])
        slabs[chunk, 4 * t] = jnp.where(even, b0, pltpu.roll(b1, 32, 1)).astype(BF)
        slabs[chunk, 4 * t + 1] = jnp.where(even, pltpu.roll(b0, 96, 1), b1).astype(BF)
        slabs[chunk, 4 * t + 2] = jnp.where(even, b2, pltpu.roll(b3, 32, 1)).astype(BF)
        slabs[chunk, 4 * t + 3] = jnp.where(even, pltpu.roll(b2, 96, 1), b3).astype(BF)


def kernel(n_lon, n_lat, *refs):
    (
        tok_h, first_h, gain1_h, wq1_h, wo1_h, second_h, gain2_h, wq2_h, wo2_h,
        high_h, north_h, low_h, gainm_h, wm_h, circle_h,
        out,
        tok, first, gain1, wq1, wo1, second, gain2, wq2, wo2,
        high, north, low, gainm, wm, circle,
        padded, x1, qkv, ones, east, x2, twos, above, slabs, inbox,
        load_sem, west_s, west_r, lat_s, lat_r, box_s, box_r,
    ) = refs
    lon = lax.axis_index("lon")
    lat = lax.axis_index("lat")
    west = lax.rem(lon + n_lon - 1, n_lon)
    up = lax.rem(lat + n_lat - 1, n_lat)
    down = lax.rem(lat + 1, n_lat)
    eastward = lax.rem(lon + 1, n_lon)

    sources = (tok_h, first_h, gain1_h, wq1_h, wo1_h, second_h, gain2_h, wq2_h, wo2_h,
               high_h, north_h, low_h, gainm_h, wm_h, circle_h)
    places = (tok, first, gain1, wq1, wo1, second, gain2, wq2, wo2,
              high, north, low, gainm, wm, circle)
    loads = [pltpu.make_async_copy(s, p, load_sem.at[n]) for n, (s, p) in enumerate(zip(sources, places))]
    for load in loads:
        load.start()
    (l_tok, l_first, l_gain1, l_wq1, l_wo1, l_second, l_gain2, l_wq2, l_wo2,
     l_high, l_north, l_low, l_gainm, l_wm, l_circle) = loads

    barrier = pltpu.get_barrier_semaphore()

    def greet(t, carry):
        pl.semaphore_signal(
            barrier, inc=1, device_id={"lon": lax.rem(lon + t, n_lon), "lat": lat}, device_id_type=MESH
        )
        return carry

    lax.fori_loop(1, n_lon, greet, 0)
    for there in ((lon, up), (west, up), (lon, down), (eastward, down)):
        pl.semaphore_signal(
            barrier, inc=1, device_id={"lon": there[0], "lat": there[1]}, device_id_type=MESH
        )

    ones[WINDOWS, 0:WEST, :] = jnp.zeros((WEST, D), BF)
    east[WINDOWS, 32:WEST, :] = jnp.zeros((WEST - 32, D), BF)
    padded[:, 16:32, :] = jnp.zeros((12, 16, D), BF)

    l_tok.wait()
    padded[:, 0:30, :] = tok[...]
    l_first.wait()
    x1[...] = dot(first[...], padded[...].reshape(12 * 32, D))
    l_gain1.wait()
    normed = layer_norm(x1[...], gain1[...])
    l_wq1.wait()
    for n in range(3):
        qkv[:, n * D : n * D + D] = dot(normed, wq1[:, n * D : n * D + D]).astype(BF)
    l_wo1.wait()

    def remote(source, target, send, recv, there):
        return pltpu.make_async_remote_copy(
            src_ref=source,
            dst_ref=target,
            send_sem=send,
            recv_sem=recv,
            device_id={"lon": there[0], "lat": there[1]},
            device_id_type=MESH,
        )

    lane = lax.broadcasted_iota(jnp.int32, (SLOTS, 128), 1)
    row = lax.broadcasted_iota(jnp.int32, (SLOTS, 128), 0)
    inside = lane < 72
    halo = {
        w: remote(ones.at[w, pl.ds(0, WEST)], east.at[w], west_s.at[w], west_r.at[w], (west, lat))
        for w in range(WINDOWS)
    }
    north_own = remote(
        ones.at[0, pl.ds(48, 32)], ones.at[WINDOWS, pl.ds(48, 32)], lat_s.at[0], lat_r.at[0], (lon, up)
    )
    north_west = remote(
        ones.at[0, pl.ds(0, 32)], east.at[WINDOWS, pl.ds(0, 32)], lat_s.at[1], lat_r.at[1], (west, up)
    )
    back = remote(twos.at[4, pl.ds(32, 48)], above, lat_s.at[2], lat_r.at[2], (lon, down))

    for step, w in enumerate((0, 4, 3, 2, 1)):
        mixed = attend(qkv, w * SLOTS, inside)
        block = x1[w * SLOTS : (w + 1) * SLOTS, :] + dot(mixed, wo1[...])
        ones[w] = block.astype(BF)
        if step == 0:
            pl.semaphore_wait(barrier, n_lon - 1 + 4)
            north_own.start()
            north_west.start()
        halo[w].start()

    l_second.wait()
    l_gain2.wait()
    l_wq2.wait()
    l_wo2.wait()
    arrived = set()
    for group in ((4, 3, 2), (1, 0)):
        for w in group:
            for need in (w, w + 1):
                if need in arrived:
                    continue
                arrived.add(need)
                if need == WINDOWS:
                    north_own.wait_recv()
                    north_west.wait_recv()
                else:
                    halo[need].wait_recv()
            x2[w * SLOTS : (w + 1) * SLOTS, :] = dot(
                second[:, 0 : 2 * SLOTS], ones[w : w + 2].reshape(2 * SLOTS, D)
            ) + dot(second[:, 2 * SLOTS :], east[w : w + 2].reshape(2 * WEST, D))
        span = slice(min(group) * SLOTS, (max(group) + 1) * SLOTS)
        normed = layer_norm(x2[span, :], gain2[...])
        for n in range(3):
            qkv[span, n * D : n * D + D] = dot(normed, wq2[:, n * D : n * D + D]).astype(BF)
        for w in group:
            allowed = inside
            if w == 4:
                open_all = lat != n_lat - 1
                allowed = inside & (((row < 36) == (lane < 36)) | open_all)
            mixed = attend(qkv, w * SLOTS, allowed)
            block = x2[w * SLOTS : (w + 1) * SLOTS, :] + dot(mixed, wo2[...])
            twos[w] = block.astype(BF)
            if w == 4:
                back.start()
        if group[0] == 4:
            l_high.wait()
            l_gainm.wait()
            l_wm.wait()
            quads = dot(high[...], twos[2:5].reshape(3 * SLOTS, D))
            chunk = 1
        else:
            back.wait_recv()
            l_north.wait()
            l_low.wait()
            quads = dot(north[...], above[...]) + dot(low[...], twos[0:3].reshape(3 * SLOTS, D))
            chunk = 0
        quads = quads.reshape(4, 64, D)
        center = jnp.sum(jnp.sum(quads, axis=0), axis=-1, keepdims=True) / (4 * D)
        apart = quads - center[None]
        spread = jnp.sum(jnp.sum(apart * apart, axis=0), axis=-1, keepdims=True) / (4 * D)
        scaled = apart * lax.rsqrt(spread + 1e-05)[None]
        normed = [(scaled[q] * gainm[:, q * D : q * D + D]).astype(BF) for q in range(4)]
        normed = jnp.concatenate(normed, axis=1)
        spread_out(dot(normed, wm[...]), slabs, chunk)

        def send(t, carry, chunk=chunk):
            there = lax.rem(lon + t, n_lon)
            remote(
                slabs.at[chunk, there], inbox.at[chunk, lon], box_s.at[chunk, there], box_r.at[chunk, lon],
                (there, lat),
            ).start()
            return carry

        lax.fori_loop(1, n_lon, send, 0)
        inbox[chunk, lon] = slabs[chunk, lon]

    l_circle.wait()
    for chunk in (1, 0):

        def receive(t, carry, chunk=chunk):
            there = lax.rem(lon + n_lon - t, n_lon)
            remote(
                slabs.at[chunk, there], inbox.at[chunk, there], box_s.at[chunk, there], box_r.at[chunk, there],
                (there, lat),
            ).wait_recv()
            return carry

        lax.fori_loop(1, n_lon, receive, 0)
        held = inbox[chunk].reshape(n_lon * 16, 128)
        laid = lax.dot_general(held, circle[...], (((0,), (0,)), ((), ())), preferred_element_type=F32)
        laid = laid.astype(BF)
        for i in range(8 if chunk == 0 else 7):
            half, v = divmod(i, 4)
            out[chunk * 8 + i] = laid[v * FEATS : (v + 1) * FEATS, half * 256 : half * 256 + 192]

    for w in range(WINDOWS):
        halo[w].wait_send()
    for copy in (north_own, north_west, back):
        copy.wait_send()

    def sent(t, carry):
        there = lax.rem(lon + t, n_lon)
        for chunk in range(2):
            remote(
                slabs.at[chunk, there], inbox.at[chunk, lon], box_s.at[chunk, there], box_r.at[chunk, lon],
                (there, lat),
            ).wait_send()
        return carry

    lax.fori_loop(1, n_lon, sent, 0)


def solution(mesh):
    n_lon, n_lat = mesh.shape["lon"], mesh.shape["lat"]

    def local(tokens, gain_one, w_qkv_one, w_out_one, gain_two, w_qkv_two, w_out_two, merge_gain, w_merge):
        first, second, high, north, low, circle = tables(n_lon)
        operands = (
            jnp.swapaxes(tokens, 0, 1), first, gain_one.reshape(1, D), w_qkv_one, w_out_one, second,
            gain_two.reshape(1, D), w_qkv_two, w_out_two, high, north, low,
            merge_gain.reshape(1, 4 * D), w_merge, circle,
        )
        out = pl.pallas_call(
            functools.partial(kernel, n_lon, n_lat),
            out_shape=jax.ShapeDtypeStruct((15, FEATS, 6 * n_lon), BF),
            in_specs=[pl.BlockSpec(memory_space=pl.ANY)] * len(operands),
            out_specs=pl.BlockSpec(memory_space=pltpu.VMEM),
            scratch_shapes=[pltpu.VMEM(o.shape, o.dtype) for o in operands]
            + [
                pltpu.VMEM((12, 32, D), BF),
                pltpu.VMEM((WINDOWS * SLOTS, D), F32),
                pltpu.VMEM((WINDOWS * SLOTS, 3 * D), BF),
                pltpu.VMEM((WINDOWS + 1, SLOTS, D), BF),
                pltpu.VMEM((WINDOWS + 1, WEST, D), BF),
                pltpu.VMEM((WINDOWS * SLOTS, D), F32),
                pltpu.VMEM((WINDOWS, SLOTS, D), BF),
                pltpu.VMEM((WEST, D), BF),
                pltpu.VMEM((2, n_lon, 16, 128), BF),
                pltpu.VMEM((2, n_lon, 16, 128), BF),
                pltpu.SemaphoreType.DMA((len(operands),)),
                pltpu.SemaphoreType.DMA((WINDOWS,)),
                pltpu.SemaphoreType.DMA((WINDOWS,)),
                pltpu.SemaphoreType.DMA((3,)),
                pltpu.SemaphoreType.DMA((3,)),
                pltpu.SemaphoreType.DMA((2, n_lon)),
                pltpu.SemaphoreType.DMA((2, n_lon)),
            ],
            compiler_params=pltpu.CompilerParams(
                collective_id=0, has_side_effects=True, vmem_limit_bytes=48 * 1024 * 1024
            ),
        )(*operands)
        return jnp.swapaxes(out, 1, 2)[None]

    return jax.shard_map(
        local,
        mesh=mesh,
        in_specs=(P("lat", "lon", None), P(), P(), P(), P(), P(), P(), P(), P()),
        out_specs=P("lat", None, None, "lon"),
        check_vma=False,
    )
```

```python
import functools

import jax
import jax.numpy as jnp
import numpy as np
from jax import lax
from jax.experimental import pallas as pl
from jax.experimental.pallas import tpu as pltpu
from jax.sharding import PartitionSpec as P

MESH = pl.DeviceIdType.MESH
BF = jnp.bfloat16
F32 = jnp.float32

D = 512
SLOTS = 80
WINDOWS = 5
LOG2E = 1.4426950408889634
WEST = 48
FEATS = 32


def tables(n_lon):
    first = np.zeros((WINDOWS * SLOTS, 12 * 32), np.float32)
    for w in range(WINDOWS):
        for r in range(6):
            for c in range(12):
                if c < 6:
                    slot = (0 if r < 3 else 18) + (r % 3) * 6 + c
                else:
                    slot = (54 if r < 3 else 36) + (r % 3) * 6 + c - 6
                first[w * SLOTS + slot, c * 32 + 6 * w + r] = 1
    second = np.zeros((SLOTS, 2 * SLOTS + 2 * WEST), np.float32)
    for r in range(6):
        for c in range(12):
            within = (r % 3) * 6 + c % 6
            if c < 6:
                source = 36 + within if r < 3 else SLOTS + 54 + within
            else:
                source = 2 * SLOTS + (18 + within if r < 3 else WEST + within)
            second[r * 12 + c, source] = 1
    high = np.zeros((256, 3 * SLOTS), np.float32)
    north = np.zeros((256, WEST), np.float32)
    low = np.zeros((256, 3 * SLOTS), np.float32)
    for corner in range(4):
        for i in range(15):
            for j in range(6):
                row = 2 * i + corner % 2
                col = 2 * j + corner // 2
                spot = corner * 64 + (i % 8) * 8 + j
                if row < 3:
                    north[spot, 4 + row * 12 + col] = 1
                    continue
                w, r = divmod(row - 3, 6)
                if i >= 8:
                    high[spot, (w - 2) * SLOTS + r * 12 + col] = 1
                else:
                    low[spot, w * SLOTS + r * 12 + col] = 1
    circle = np.zeros((n_lon * 16, 512), np.float32)
    for s in range(n_lon):
        for half in range(2):
            for j in range(6):
                circle[s * 16 + half * 8 + j, half * 256 + (6 * s + 3 + j) % (6 * n_lon)] = 1
    return [jnp.asarray(t, BF) for t in (first, second, high, north, low, circle)]


def dot(a, b):
    return jnp.dot(a, b, preferred_element_type=F32)


def dot_t(a, b):
    return lax.dot_general(a, b, (((1,), (1,)), ((), ())), preferred_element_type=F32)


def layer_norm(x, gain):
    center = jnp.mean(x, axis=-1, keepdims=True)
    d = x - center
    spread = jnp.mean(d * d, axis=-1, keepdims=True)
    return (d * lax.rsqrt(spread + 1e-05) * gain).astype(BF)


def by_head(block):
    lane = lax.broadcasted_iota(jnp.int32, block.shape, 1) // 64
    empty = jnp.zeros((128 - SLOTS, 256), BF)
    parts = []
    for h in range(4):
        parts += [jnp.where(lane == h, block, jnp.zeros_like(block)), empty]
    return jnp.concatenate(parts, axis=0)


def attend(qkv, bases, masks):
    def scores(base):
        rows = pl.ds(base, SLOTS)
        k = qkv[rows, D : 2 * D]
        stacks = []
        for g in range(2):
            q = qkv[rows, g * 256 : g * 256 + 256]
            lane = lax.broadcasted_iota(jnp.int32, q.shape, 1) // 64
            stacks.append(jnp.concatenate([jnp.where(lane == h, q, jnp.zeros_like(q)) for h in range(4)], axis=0))
        low, high = k[:, 0:256], k[:, 256:512]
        return jnp.concatenate(
            [
                dot_t(low, stacks[0][0:256]),
                dot_t(low, jnp.concatenate([stacks[0][256:320], jnp.zeros((192, 256), BF)], axis=0))
                + dot_t(high, jnp.concatenate([jnp.zeros((64, 256), BF), stacks[1][0:192]], axis=0)),
                dot_t(high, stacks[1][192:320]),
            ],
            axis=1,
        )[0:72]

    def softmax(s, mask):
        if mask is not None:
            s = jnp.where(mask, s, -1e30)
        top = jnp.max(s, axis=0, keepdims=True)
        expo = jnp.exp2((s - top) * (0.125 * LOG2E))
        total = jnp.sum(expo, axis=0, keepdims=True)
        probs = expo * (1.0 / total)
        padded = jnp.concatenate([probs, jnp.zeros((56, 8 * SLOTS), F32)], axis=0)
        return padded.astype(BF).T

    def mix(probs, base):
        mixed = []
        for g in range(2):
            at = 2 * D + g * 256
            v = by_head(qkv[pl.ds(base, SLOTS), at : at + 256])
            wide = jnp.concatenate([probs[(4 * g + h) * SLOTS : (4 * g + h + 1) * SLOTS] for h in range(4)], axis=1)
            mixed.append(dot(wide, v).astype(BF))
        return jnp.concatenate(mixed, axis=1)

    count = len(bases)
    mixed, s, probs = [], scores(bases[0]), None
    for n in range(count):
        following = scores(bases[n + 1]) if n + 1 < count else None
        if probs is not None:
            mixed.append(mix(probs, bases[n - 1]))
        probs = softmax(s, masks[n])
        s = following
    mixed.append(mix(probs, bases[-1]))
    return mixed


def spread_out(result, slabs, chunk):
    parts = result.reshape(2, 4, 8, 1024)
    lane = lax.broadcasted_iota(jnp.int32, (16, 128), 1)
    left = lane < 64
    even = (lane // 32) % 2 == 0
    for t in range(8):
        a = [parts[:, v, :, t * 128 : t * 128 + 128].reshape(16, 128) for v in range(4)]
        b0 = jnp.where(left, a[0], pltpu.roll(a[2], 64, 1))
        b1 = jnp.where(left, a[1], pltpu.roll(a[3], 64, 1))
        b2 = jnp.where(left, pltpu.roll(a[0], 64, 1), a[2])
        b3 = jnp.where(left, pltpu.roll(a[1], 64, 1), a[3])
        slabs[chunk, 4 * t] = jnp.where(even, b0, pltpu.roll(b1, 32, 1)).astype(BF)
        slabs[chunk, 4 * t + 1] = jnp.where(even, pltpu.roll(b0, 96, 1), b1).astype(BF)
        slabs[chunk, 4 * t + 2] = jnp.where(even, b2, pltpu.roll(b3, 32, 1)).astype(BF)
        slabs[chunk, 4 * t + 3] = jnp.where(even, pltpu.roll(b2, 96, 1), b3).astype(BF)


def kernel(n_lon, n_lat, *refs):
    (
        tok_h, first_h, gain1_h, wq1_h, wo1_h, second_h, gain2_h, wq2_h, wo2_h,
        high_h, north_h, low_h, gainm_h, wm_h, circle_h,
        out,
        tok, first, gain1, wq1, wo1, second, gain2, wq2, wo2,
        high, north, low, gainm, wm, circle,
        padded, x1, qkv, ones, east, x2, twos, above, slabs, inbox,
        load_sem, west_s, west_r, lat_s, lat_r, box_s, box_r,
    ) = refs
    lon = lax.axis_index("lon")
    lat = lax.axis_index("lat")
    west = lax.rem(lon + n_lon - 1, n_lon)
    up = lax.rem(lat + n_lat - 1, n_lat)
    down = lax.rem(lat + 1, n_lat)
    eastward = lax.rem(lon + 1, n_lon)

    sources = (tok_h, first_h, gain1_h, wq1_h, wo1_h, second_h, gain2_h, wq2_h, wo2_h,
               high_h, north_h, low_h, gainm_h, wm_h, circle_h)
    places = (tok, first, gain1, wq1, wo1, second, gain2, wq2, wo2,
              high, north, low, gainm, wm, circle)
    loads = [pltpu.make_async_copy(s, p, load_sem.at[n]) for n, (s, p) in enumerate(zip(sources, places))]
    (l_tok, l_first, l_gain1, l_wq1, l_wo1, l_second, l_gain2, l_wq2, l_wo2,
     l_high, l_north, l_low, l_gainm, l_wm, l_circle) = loads
    for load in (l_tok, l_first, l_gain1, l_wq1):
        load.start()

    barrier = pltpu.get_barrier_semaphore()

    def greet(t, carry):
        pl.semaphore_signal(
            barrier, inc=1, device_id={"lon": lax.rem(lon + t, n_lon), "lat": lat}, device_id_type=MESH
        )
        return carry

    lax.fori_loop(1, n_lon, greet, 0)
    for there in ((lon, up), (west, up), (lon, down), (eastward, down)):
        pl.semaphore_signal(
            barrier, inc=1, device_id={"lon": there[0], "lat": there[1]}, device_id_type=MESH
        )

    ones[WINDOWS, 0:WEST, :] = jnp.zeros((WEST, D), BF)
    east[WINDOWS, 32:WEST, :] = jnp.zeros((WEST - 32, D), BF)
    padded[:, 16:32, :] = jnp.zeros((12, 16, D), BF)

    l_tok.wait()
    padded[:, 0:30, :] = tok[...]
    l_first.wait()
    x1[...] = dot(first[...], padded[...].reshape(12 * 32, D))
    l_gain1.wait()
    normed = layer_norm(x1[...], gain1[...])
    l_wq1.wait()
    for load in (l_wo1, l_second, l_gain2, l_wq2, l_wo2, l_wm, l_high, l_gainm, l_north, l_low, l_circle):
        load.start()
    for n in range(3):
        qkv[:, n * D : n * D + D] = dot(normed, wq1[:, n * D : n * D + D]).astype(BF)
    l_wo1.wait()

    def remote(source, target, send, recv, there):
        return pltpu.make_async_remote_copy(
            src_ref=source,
            dst_ref=target,
            send_sem=send,
            recv_sem=recv,
            device_id={"lon": there[0], "lat": there[1]},
            device_id_type=MESH,
        )

    key = lax.broadcasted_iota(jnp.int32, (72, 8 * SLOTS), 0)
    query = lax.broadcasted_iota(jnp.int32, (72, 8 * SLOTS), 1) % SLOTS
    halo = {
        w: remote(ones.at[w, pl.ds(0, WEST)], east.at[w], west_s.at[w], west_r.at[w], (west, lat))
        for w in range(WINDOWS)
    }
    north_own = remote(
        ones.at[0, pl.ds(48, 32)], ones.at[WINDOWS, pl.ds(48, 32)], lat_s.at[0], lat_r.at[0], (lon, up)
    )
    north_west = remote(
        ones.at[0, pl.ds(0, 32)], east.at[WINDOWS, pl.ds(0, 32)], lat_s.at[1], lat_r.at[1], (west, up)
    )
    back = remote(twos.at[4, pl.ds(32, 48)], above, lat_s.at[2], lat_r.at[2], (lon, down))

    def first_block(order):
        mixed = attend(qkv, [w * SLOTS for w in order], [None] * len(order))
        update = dot(jnp.concatenate(mixed, axis=0), wo1[...])
        for n, w in enumerate(order):
            block = x1[w * SLOTS : (w + 1) * SLOTS, :] + update[n * SLOTS : (n + 1) * SLOTS]
            ones[w] = block.astype(BF)

    first_block((0, 4))
    pl.semaphore_wait(barrier, n_lon - 1 + 4)
    north_own.start()
    north_west.start()
    halo[4].start()
    halo[0].start()
    first_block((3, 2))
    halo[3].start()
    halo[2].start()
    first_block((1,))
    halo[1].start()
    l_second.wait()
    l_gain2.wait()
    l_wq2.wait()
    l_wo2.wait()
    def gather(w):
        x2[w * SLOTS : (w + 1) * SLOTS, :] = dot(
            second[:, 0 : 2 * SLOTS], ones[w : w + 2].reshape(2 * SLOTS, D)
        ) + dot(second[:, 2 * SLOTS :], east[w : w + 2].reshape(2 * WEST, D))

    def project(first_w, last_w):
        span = slice(first_w * SLOTS, (last_w + 1) * SLOTS)
        normed = layer_norm(x2[span, :], gain2[...])
        for n in range(3):
            qkv[span, n * D : n * D + D] = dot(normed, wq2[:, n * D : n * D + D]).astype(BF)

    def finish(order, masks):
        mixed = attend(qkv, [w * SLOTS for w in order], masks)
        update = dot(jnp.concatenate(mixed, axis=0), wo2[...])
        for n, w in enumerate(order):
            block = x2[w * SLOTS : (w + 1) * SLOTS, :] + update[n * SLOTS : (n + 1) * SLOTS]
            twos[w] = block.astype(BF)

    def merge(quads, chunk):
        quads = quads.reshape(4, 64, D)
        center = jnp.sum(jnp.sum(quads, axis=0), axis=-1, keepdims=True) / (4 * D)
        apart = quads - center[None]
        spread = jnp.sum(jnp.sum(apart * apart, axis=0), axis=-1, keepdims=True) / (4 * D)
        scaled = apart * lax.rsqrt(spread + 1e-05)[None]
        normed = [(scaled[q] * gainm[:, q * D : q * D + D]).astype(BF) for q in range(4)]
        spread_out(dot(jnp.concatenate(normed, axis=1), wm[...]), slabs, chunk)

    def parcels(chunk):
        return remote(
            slabs.at[chunk, pl.ds(0, n_lon - 1)], inbox.at[chunk, pl.ds(0, n_lon - 1)], box_s.at[chunk], box_r.at[chunk],
            (west, lat),
        )

    def hand_out(chunk):
        def send(t, carry):
            there = lax.rem(lon + t, n_lon)
            remote(
                slabs.at[chunk, there], inbox.at[chunk, lon], box_s.at[chunk], box_r.at[chunk], (there, lat)
            ).start()
            return carry

        lax.fori_loop(1, n_lon, send, 0)
        inbox[chunk, lon] = slabs[chunk, lon]

    for w in (4, 3, 2):
        halo[w].wait_recv()
    north_own.wait_recv()
    north_west.wait_recv()
    for w in (4, 3, 2):
        gather(w)
    project(2, 4)
    parted = ((key < 36) == (query < 36)) | (lat != n_lat - 1)
    finish((4,), [parted])
    back.start()
    finish((3, 2), [None, None])
    l_high.wait()
    l_gainm.wait()
    l_wm.wait()
    merge(dot(high[...], twos[2:5].reshape(3 * SLOTS, D)), 1)
    hand_out(1)
    halo[1].wait_recv()
    halo[0].wait_recv()
    gather(1)
    gather(0)
    project(0, 1)
    finish((1, 0), [None, None])
    back.wait_recv()
    l_north.wait()
    l_low.wait()
    merge(dot(north[...], above[...]) + dot(low[...], twos[0:3].reshape(3 * SLOTS, D)), 0)
    hand_out(0)

    l_circle.wait()
    for chunk in (1, 0):
        parcels(chunk).wait_recv()
        held = inbox[chunk].reshape(n_lon * 16, 128)
        laid = lax.dot_general(held, circle[...], (((0,), (0,)), ((), ())), preferred_element_type=F32)
        laid = laid.astype(BF)
        for i in range(8 if chunk == 0 else 7):
            half, v = divmod(i, 4)
            out[chunk * 8 + i] = laid[v * FEATS : (v + 1) * FEATS, half * 256 : half * 256 + 192]

    for w in range(WINDOWS):
        halo[w].wait_send()
    for copy in (north_own, north_west, back):
        copy.wait_send()

    for chunk in range(2):
        parcels(chunk).wait_send()


def solution(mesh):
    n_lon, n_lat = mesh.shape["lon"], mesh.shape["lat"]

    def local(tokens, gain_one, w_qkv_one, w_out_one, gain_two, w_qkv_two, w_out_two, merge_gain, w_merge):
        first, second, high, north, low, circle = tables(n_lon)
        operands = (
            jnp.swapaxes(tokens, 0, 1), first, gain_one.reshape(1, D), w_qkv_one, w_out_one, second,
            gain_two.reshape(1, D), w_qkv_two, w_out_two, high, north, low,
            merge_gain.reshape(1, 4 * D), w_merge, circle,
        )
        out = pl.pallas_call(
            functools.partial(kernel, n_lon, n_lat),
            out_shape=pltpu.VMEM((15, FEATS, 6 * n_lon), BF),
            in_specs=[pl.BlockSpec(memory_space=pltpu.HBM)] * len(operands),
            out_specs=pl.BlockSpec(memory_space=pltpu.VMEM),
            scratch_shapes=[pltpu.VMEM(o.shape, o.dtype) for o in operands]
            + [
                pltpu.VMEM((12, 32, D), BF),
                pltpu.VMEM((WINDOWS * SLOTS, D), F32),
                pltpu.VMEM((WINDOWS * SLOTS, 3 * D), BF),
                pltpu.VMEM((WINDOWS + 1, SLOTS, D), BF),
                pltpu.VMEM((WINDOWS + 1, WEST, D), BF),
                pltpu.VMEM((WINDOWS * SLOTS, D), F32),
                pltpu.VMEM((WINDOWS, SLOTS, D), BF),
                pltpu.VMEM((WEST, D), BF),
                pltpu.VMEM((2, n_lon, 16, 128), BF),
                pltpu.VMEM((2, n_lon, 16, 128), BF),
                pltpu.SemaphoreType.DMA((len(operands),)),
                pltpu.SemaphoreType.DMA((WINDOWS,)),
                pltpu.SemaphoreType.DMA((WINDOWS,)),
                pltpu.SemaphoreType.DMA((3,)),
                pltpu.SemaphoreType.DMA((3,)),
                pltpu.SemaphoreType.DMA((2,)),
                pltpu.SemaphoreType.DMA((2,)),
            ],
            compiler_params=pltpu.CompilerParams(
                collective_id=0, has_side_effects=True, vmem_limit_bytes=56 * 1024 * 1024
            ),
        )(*operands)
        return jnp.swapaxes(out, 1, 2)[None]

    return jax.shard_map(
        local,
        mesh=mesh,
        in_specs=(P("lat", "lon", None), P(), P(), P(), P(), P(), P(), P(), P()),
        out_specs=P("lat", None, None, "lon"),
        check_vma=False,
    )
```

```python
import functools

import jax
import jax.numpy as jnp
import numpy as np
from jax import lax
from jax.experimental import pallas as pl
from jax.experimental.pallas import tpu as pltpu
from jax.sharding import PartitionSpec as P

MESH = pl.DeviceIdType.MESH
BF = jnp.bfloat16
F32 = jnp.float32

D = 512
SLOTS = 80
WINDOWS = 5
LOG2E = 1.4426950408889634
WEST = 48
FEATS = 32


def tables(n_lon):
    first = np.zeros((WINDOWS * SLOTS, 12 * 32), np.float32)
    for w in range(WINDOWS):
        for r in range(6):
            for c in range(12):
                if c < 6:
                    slot = (0 if r < 3 else 18) + (r % 3) * 6 + c
                else:
                    slot = (54 if r < 3 else 36) + (r % 3) * 6 + c - 6
                first[w * SLOTS + slot, c * 32 + 6 * w + r] = 1
    second = np.zeros((SLOTS, 2 * SLOTS + 2 * WEST), np.float32)
    for r in range(6):
        for c in range(12):
            within = (r % 3) * 6 + c % 6
            if c < 6:
                source = 36 + within if r < 3 else SLOTS + 54 + within
            else:
                source = 2 * SLOTS + (18 + within if r < 3 else WEST + within)
            second[r * 12 + c, source] = 1
    high = np.zeros((256, 3 * SLOTS), np.float32)
    north = np.zeros((256, WEST), np.float32)
    low = np.zeros((256, 3 * SLOTS), np.float32)
    for corner in range(4):
        for i in range(15):
            for j in range(6):
                row = 2 * i + corner % 2
                col = 2 * j + corner // 2
                spot = corner * 64 + (i % 8) * 8 + j
                if row < 3:
                    north[spot, 4 + row * 12 + col] = 1
                    continue
                w, r = divmod(row - 3, 6)
                if i >= 8:
                    high[spot, (w - 2) * SLOTS + r * 12 + col] = 1
                else:
                    low[spot, w * SLOTS + r * 12 + col] = 1
    circle = np.zeros((n_lon * 16, 512), np.float32)
    for s in range(n_lon):
        for half in range(2):
            for j in range(6):
                circle[s * 16 + half * 8 + j, half * 256 + (6 * s + 3 + j) % (6 * n_lon)] = 1
    return [jnp.asarray(t, BF) for t in (first, second, high, north, low, circle)]


def dot(a, b):
    return jnp.dot(a, b, preferred_element_type=F32)


def dot_t(a, b):
    return lax.dot_general(a, b, (((1,), (1,)), ((), ())), preferred_element_type=F32)


def layer_norm(x, gain):
    center = jnp.mean(x, axis=-1, keepdims=True)
    d = x - center
    spread = jnp.mean(d * d, axis=-1, keepdims=True)
    return (d * lax.rsqrt(spread + 1e-05) * gain).astype(BF)


def by_head(block):
    lane = lax.broadcasted_iota(jnp.int32, block.shape, 1) // 64
    empty = jnp.zeros((128 - SLOTS, 256), BF)
    parts = []
    for h in range(4):
        parts += [jnp.where(lane == h, block, jnp.zeros_like(block)), empty]
    return jnp.concatenate(parts, axis=0)


def attend(qkv, bases, masks):
    def scores(base):
        rows = pl.ds(base, SLOTS)
        k = qkv[rows, D : 2 * D]
        stacks = []
        for g in range(2):
            q = qkv[rows, g * 256 : g * 256 + 256]
            lane = lax.broadcasted_iota(jnp.int32, q.shape, 1) // 64
            stacks.append(jnp.concatenate([jnp.where(lane == h, q, jnp.zeros_like(q)) for h in range(4)], axis=0))
        low, high = k[:, 0:256], k[:, 256:512]
        return jnp.concatenate(
            [
                dot_t(low, stacks[0][0:256]),
                dot_t(low, jnp.concatenate([stacks[0][256:320], jnp.zeros((192, 256), BF)], axis=0))
                + dot_t(high, jnp.concatenate([jnp.zeros((64, 256), BF), stacks[1][0:192]], axis=0)),
                dot_t(high, stacks[1][192:320]),
            ],
            axis=1,
        )[0:72]

    def softmax(s, mask):
        if mask is not None:
            s = jnp.where(mask, s, -1e30)
        top = jnp.max(s, axis=0, keepdims=True)
        expo = jnp.exp2((s - top) * (0.125 * LOG2E))
        total = jnp.sum(expo, axis=0, keepdims=True)
        probs = expo * (1.0 / total)
        padded = jnp.concatenate([probs, jnp.zeros((56, 8 * SLOTS), F32)], axis=0)
        return padded.astype(BF).T

    def mix(probs, base):
        mixed = []
        for g in range(2):
            at = 2 * D + g * 256
            v = by_head(qkv[pl.ds(base, SLOTS), at : at + 256])
            wide = jnp.concatenate([probs[(4 * g + h) * SLOTS : (4 * g + h + 1) * SLOTS] for h in range(4)], axis=1)
            mixed.append(dot(wide, v).astype(BF))
        return jnp.concatenate(mixed, axis=1)

    count = len(bases)
    mixed, s, probs = [], scores(bases[0]), None
    for n in range(count):
        following = scores(bases[n + 1]) if n + 1 < count else None
        if probs is not None:
            mixed.append(mix(probs, bases[n - 1]))
        probs = softmax(s, masks[n])
        s = following
    mixed.append(mix(probs, bases[-1]))
    return mixed


def spread_out(result, slabs, chunk, base):
    parts = result.reshape(2, 4, 8, 256)
    lane = lax.broadcasted_iota(jnp.int32, (16, 128), 1)
    left = lane < 64
    even = (lane // 32) % 2 == 0
    for t in range(2):
        a = [parts[:, v, :, t * 128 : t * 128 + 128].reshape(16, 128) for v in range(4)]
        b0 = jnp.where(left, a[0], pltpu.roll(a[2], 64, 1))
        b1 = jnp.where(left, a[1], pltpu.roll(a[3], 64, 1))
        b2 = jnp.where(left, pltpu.roll(a[0], 64, 1), a[2])
        b3 = jnp.where(left, pltpu.roll(a[1], 64, 1), a[3])
        slabs[chunk, base + 4 * t] = jnp.where(even, b0, pltpu.roll(b1, 32, 1)).astype(BF)
        slabs[chunk, base + 4 * t + 1] = jnp.where(even, pltpu.roll(b0, 96, 1), b1).astype(BF)
        slabs[chunk, base + 4 * t + 2] = jnp.where(even, b2, pltpu.roll(b3, 32, 1)).astype(BF)
        slabs[chunk, base + 4 * t + 3] = jnp.where(even, pltpu.roll(b2, 96, 1), b3).astype(BF)


def kernel(n_lon, n_lat, *refs):
    (
        tok_h, first_h, gain1_h, wq1_h, wo1_h, second_h, gain2_h, wq2_h, wo2_h,
        high_h, north_h, low_h, gainm_h, wm_h, circle_h,
        out,
        tok, first, gain1, wq1, wo1, second, gain2, wq2, wo2,
        high, north, low, gainm, wm, circle,
        padded, x1, qkv, ones, east, x2, twos, above, slabs, inbox,
        load_sem, west_s, west_r, lat_s, lat_r, box_s, box_r,
    ) = refs
    lon = lax.axis_index("lon")
    lat = lax.axis_index("lat")
    west = lax.rem(lon + n_lon - 1, n_lon)
    owners = n_lon // 4
    up = lax.rem(lat + n_lat - 1, n_lat)
    down = lax.rem(lat + 1, n_lat)
    eastward = lax.rem(lon + 1, n_lon)

    sources = (tok_h, first_h, gain1_h, wq1_h, wo1_h, second_h, gain2_h, wq2_h, wo2_h,
               high_h, north_h, low_h, gainm_h, wm_h, circle_h)
    places = (tok, first, gain1, wq1, wo1, second, gain2, wq2, wo2,
              high, north, low, gainm, wm, circle)
    loads = [pltpu.make_async_copy(s, p, load_sem.at[n]) for n, (s, p) in enumerate(zip(sources, places))]
    (l_tok, l_first, l_gain1, l_wq1, l_wo1, l_second, l_gain2, l_wq2, l_wo2,
     l_high, l_north, l_low, l_gainm, l_wm, l_circle) = loads
    for load in (l_tok, l_first, l_gain1, l_wq1):
        load.start()

    barrier = pltpu.get_barrier_semaphore()

    def greet(t, carry):
        pl.semaphore_signal(
            barrier, inc=1, device_id={"lon": lax.rem(lon + t, n_lon), "lat": lat}, device_id_type=MESH
        )
        return carry

    lax.fori_loop(1, n_lon, greet, 0)
    for there in ((lon, up), (west, up), (lon, down), (eastward, down)):
        pl.semaphore_signal(
            barrier, inc=1, device_id={"lon": there[0], "lat": there[1]}, device_id_type=MESH
        )

    ones[WINDOWS, 0:WEST, :] = jnp.zeros((WEST, D), BF)
    east[WINDOWS, 32:WEST, :] = jnp.zeros((WEST - 32, D), BF)
    padded[:, 16:32, :] = jnp.zeros((12, 16, D), BF)

    l_tok.wait()
    padded[:, 0:30, :] = tok[...]
    def first_project(order):
        picks = jnp.concatenate([first[w * SLOTS : (w + 1) * SLOTS] for w in order], axis=0)
        x = dot(picks, padded[...].reshape(12 * 32, D))
        normed = layer_norm(x, gain1[...])
        for n, w in enumerate(order):
            x1[w * SLOTS : (w + 1) * SLOTS, :] = x[n * SLOTS : (n + 1) * SLOTS]
        return normed

    def first_heads(order, normed):
        for part in range(3):
            y = dot(normed, wq1[:, part * D : part * D + D]).astype(BF)
            for n, w in enumerate(order):
                qkv[w * SLOTS : (w + 1) * SLOTS, part * D : part * D + D] = y[n * SLOTS : (n + 1) * SLOTS]

    def first_block(order):
        mixed = attend(qkv, [w * SLOTS for w in order], [None] * len(order))
        update = dot(jnp.concatenate(mixed, axis=0), wo1[...])
        for n, w in enumerate(order):
            block = x1[w * SLOTS : (w + 1) * SLOTS, :] + update[n * SLOTS : (n + 1) * SLOTS]
            ones[w] = block.astype(BF)

    def remote(source, target, send, recv, there):
        return pltpu.make_async_remote_copy(
            src_ref=source,
            dst_ref=target,
            send_sem=send,
            recv_sem=recv,
            device_id={"lon": there[0], "lat": there[1]},
            device_id_type=MESH,
        )

    key = lax.broadcasted_iota(jnp.int32, (72, 8 * SLOTS), 0)
    query = lax.broadcasted_iota(jnp.int32, (72, 8 * SLOTS), 1) % SLOTS
    halo = {
        w: remote(ones.at[w, pl.ds(0, WEST)], east.at[w], west_s.at[w], west_r.at[w], (west, lat))
        for w in range(WINDOWS)
    }
    north_own = remote(
        ones.at[0, pl.ds(48, 32)], ones.at[WINDOWS, pl.ds(48, 32)], lat_s.at[0], lat_r.at[0], (lon, up)
    )
    north_west = remote(
        ones.at[0, pl.ds(0, 32)], east.at[WINDOWS, pl.ds(0, 32)], lat_s.at[1], lat_r.at[1], (west, up)
    )
    back = remote(twos.at[4, pl.ds(32, 48)], above, lat_s.at[2], lat_r.at[2], (lon, down))

    l_first.wait()
    l_gain1.wait()
    normed = first_project((0, 4))
    l_wq1.wait()
    for load in (l_wo1, l_second, l_gain2, l_wq2, l_wo2, l_wm, l_high, l_gainm, l_north, l_low, l_circle):
        load.start()
    first_heads((0, 4), normed)
    l_wo1.wait()
    first_block((0, 4))
    pl.semaphore_wait(barrier, n_lon - 1 + 4)
    north_own.start()
    north_west.start()
    halo[4].start()
    halo[0].start()
    first_heads((3, 2, 1), first_project((3, 2, 1)))
    first_block((3, 2))
    halo[3].start()
    halo[2].start()
    first_block((1,))
    halo[1].start()
    l_second.wait()
    l_gain2.wait()
    l_wq2.wait()
    l_wo2.wait()
    def gather(w):
        x2[w * SLOTS : (w + 1) * SLOTS, :] = dot(
            second[:, 0 : 2 * SLOTS], ones[w : w + 2].reshape(2 * SLOTS, D)
        ) + dot(second[:, 2 * SLOTS :], east[w : w + 2].reshape(2 * WEST, D))

    def project(first_w, last_w):
        span = slice(first_w * SLOTS, (last_w + 1) * SLOTS)
        normed = layer_norm(x2[span, :], gain2[...])
        for n in range(3):
            qkv[span, n * D : n * D + D] = dot(normed, wq2[:, n * D : n * D + D]).astype(BF)

    def finish(order, masks):
        mixed = attend(qkv, [w * SLOTS for w in order], masks)
        update = dot(jnp.concatenate(mixed, axis=0), wo2[...])
        for n, w in enumerate(order):
            block = x2[w * SLOTS : (w + 1) * SLOTS, :] + update[n * SLOTS : (n + 1) * SLOTS]
            twos[w] = block.astype(BF)

    def merge(quads, chunk):
        quads = quads.reshape(4, 64, D)
        center = jnp.sum(jnp.sum(quads, axis=0), axis=-1, keepdims=True) / (4 * D)
        apart = quads - center[None]
        spread = jnp.sum(jnp.sum(apart * apart, axis=0), axis=-1, keepdims=True) / (4 * D)
        scaled = apart * lax.rsqrt(spread + 1e-05)[None]
        normed = [(scaled[q] * gainm[:, q * D : q * D + D]).astype(BF) for q in range(4)]
        normed = jnp.concatenate(normed, axis=1)
        def post(result, quarter, skip):
            spread_out(result, slabs, chunk, quarter * owners)
            for turn in range(skip, owners):
                beside = lon - lon // owners * owners + turn
                there = quarter * owners + jnp.where(beside >= owners, beside - owners, beside)
                remote(
                    slabs.at[chunk, there], inbox.at[chunk, lon], box_s.at[chunk], box_r.at[chunk], (there, lat)
                ).start()

        made = None
        for aside, beyond in ((1, 1), (0, 1), (1, 0), (0, 0)):
            quarter = lax.rem(lon // (2 * owners) + aside, 2) * 2 + lax.rem(lon // owners + beyond, 2)
            columns = pl.ds(pl.multiple_of(quarter * (owners * FEATS), owners * FEATS), owners * FEATS)
            result = dot(normed, wm[:, columns])
            if made is not None:
                post(*made, 0)
            made = (result, quarter)
        post(*made, 1)
        inbox[chunk, lon] = slabs[chunk, lon]

    def parcels(chunk):
        return remote(
            slabs.at[chunk, pl.ds(0, n_lon - 1)], inbox.at[chunk, pl.ds(0, n_lon - 1)], box_s.at[chunk], box_r.at[chunk],
            (west, lat),
        )

    parted = ((key < 36) == (query < 36)) | (lat != n_lat - 1)
    halo[4].wait_recv()
    north_own.wait_recv()
    north_west.wait_recv()
    gather(4)
    project(4, 4)
    finish((4,), [parted])
    back.start()
    halo[3].wait_recv()
    halo[2].wait_recv()
    gather(3)
    gather(2)
    project(2, 3)
    finish((3, 2), [None, None])
    l_high.wait()
    l_gainm.wait()
    l_wm.wait()
    merge(dot(high[...], twos[2:5].reshape(3 * SLOTS, D)), 1)
    halo[1].wait_recv()
    halo[0].wait_recv()
    gather(1)
    gather(0)
    project(0, 1)
    finish((1, 0), [None, None])
    back.wait_recv()
    l_north.wait()
    l_low.wait()
    merge(dot(north[...], above[...]) + dot(low[...], twos[0:3].reshape(3 * SLOTS, D)), 0)

    l_circle.wait()
    for chunk in (1, 0):
        parcels(chunk).wait_recv()
        held = inbox[chunk].reshape(n_lon * 16, 128)
        laid = lax.dot_general(held, circle[...], (((0,), (0,)), ((), ())), preferred_element_type=F32)
        laid = laid.astype(BF)
        for i in range(8 if chunk == 0 else 7):
            half, v = divmod(i, 4)
            out[chunk * 8 + i] = laid[v * FEATS : (v + 1) * FEATS, half * 256 : half * 256 + 192]

    for w in range(WINDOWS):
        halo[w].wait_send()
    for copy in (north_own, north_west, back):
        copy.wait_send()

    for chunk in range(2):
        parcels(chunk).wait_send()


def solution(mesh):
    n_lon, n_lat = mesh.shape["lon"], mesh.shape["lat"]

    def local(tokens, gain_one, w_qkv_one, w_out_one, gain_two, w_qkv_two, w_out_two, merge_gain, w_merge):
        first, second, high, north, low, circle = tables(n_lon)
        operands = (
            jnp.swapaxes(tokens, 0, 1), first, gain_one.reshape(1, D), w_qkv_one, w_out_one, second,
            gain_two.reshape(1, D), w_qkv_two, w_out_two, high, north, low,
            merge_gain.reshape(1, 4 * D), w_merge, circle,
        )
        out = pl.pallas_call(
            functools.partial(kernel, n_lon, n_lat),
            out_shape=pltpu.VMEM((15, FEATS, 6 * n_lon), BF),
            in_specs=[pl.BlockSpec(memory_space=pltpu.HBM)] * len(operands),
            out_specs=pl.BlockSpec(memory_space=pltpu.VMEM),
            scratch_shapes=[pltpu.VMEM(o.shape, o.dtype) for o in operands]
            + [
                pltpu.VMEM((12, 32, D), BF),
                pltpu.VMEM((WINDOWS * SLOTS, D), F32),
                pltpu.VMEM((WINDOWS * SLOTS, 3 * D), BF),
                pltpu.VMEM((WINDOWS + 1, SLOTS, D), BF),
                pltpu.VMEM((WINDOWS + 1, WEST, D), BF),
                pltpu.VMEM((WINDOWS * SLOTS, D), F32),
                pltpu.VMEM((WINDOWS, SLOTS, D), BF),
                pltpu.VMEM((WEST, D), BF),
                pltpu.VMEM((2, n_lon, 16, 128), BF),
                pltpu.VMEM((2, n_lon, 16, 128), BF),
                pltpu.SemaphoreType.DMA((len(operands),)),
                pltpu.SemaphoreType.DMA((WINDOWS,)),
                pltpu.SemaphoreType.DMA((WINDOWS,)),
                pltpu.SemaphoreType.DMA((3,)),
                pltpu.SemaphoreType.DMA((3,)),
                pltpu.SemaphoreType.DMA((2,)),
                pltpu.SemaphoreType.DMA((2,)),
            ],
            compiler_params=pltpu.CompilerParams(
                collective_id=0, has_side_effects=True, vmem_limit_bytes=56 * 1024 * 1024
            ),
        )(*operands)
        return jnp.swapaxes(out, 1, 2)[None]

    return jax.shard_map(
        local,
        mesh=mesh,
        in_specs=(P("lat", "lon", None), P(), P(), P(), P(), P(), P(), P(), P()),
        out_specs=P("lat", None, None, "lon"),
        check_vma=False,
    )
```

```python
import functools

import jax
import jax.numpy as jnp
import numpy as np
from jax import lax
from jax.experimental import pallas as pl
from jax.experimental.pallas import tpu as pltpu
from jax.sharding import PartitionSpec as P

MESH = pl.DeviceIdType.MESH
BF = jnp.bfloat16
F32 = jnp.float32

D = 512
SLOTS = 80
WINDOWS = 5
LOG2E = 1.4426950408889634
WEST = 48
FEATS = 32


def tables(n_lon):
    first = np.zeros((WINDOWS * SLOTS, 12 * 32), np.float32)
    for w in range(WINDOWS):
        for r in range(6):
            for c in range(12):
                if c < 6:
                    slot = (0 if r < 3 else 18) + (r % 3) * 6 + c
                else:
                    slot = (54 if r < 3 else 36) + (r % 3) * 6 + c - 6
                first[w * SLOTS + slot, c * 32 + 6 * w + r] = 1
    second = np.zeros((SLOTS, 2 * SLOTS + 2 * WEST), np.float32)
    for r in range(6):
        for c in range(12):
            within = (r % 3) * 6 + c % 6
            if c < 6:
                source = 36 + within if r < 3 else SLOTS + 54 + within
            else:
                source = 2 * SLOTS + (18 + within if r < 3 else WEST + within)
            second[r * 12 + c, source] = 1
    high = np.zeros((256, 3 * SLOTS), np.float32)
    north = np.zeros((256, WEST), np.float32)
    low = np.zeros((256, 3 * SLOTS), np.float32)
    for corner in range(4):
        for i in range(15):
            for j in range(6):
                row = 2 * i + corner % 2
                col = 2 * j + corner // 2
                spot = corner * 64 + (i % 8) * 8 + j
                if row < 3:
                    north[spot, 4 + row * 12 + col] = 1
                    continue
                w, r = divmod(row - 3, 6)
                if i >= 8:
                    high[spot, (w - 2) * SLOTS + r * 12 + col] = 1
                else:
                    low[spot, w * SLOTS + r * 12 + col] = 1
    circle = np.zeros((n_lon * 16, 512), np.float32)
    for s in range(n_lon):
        for half in range(2):
            for j in range(6):
                circle[s * 16 + half * 8 + j, half * 256 + (6 * s + 3 + j) % (6 * n_lon)] = 1
    return [jnp.asarray(t, BF) for t in (first, second, high, north, low, circle)]


def dot(a, b):
    return jnp.dot(a, b, preferred_element_type=F32)


def dot_t(a, b):
    return lax.dot_general(a, b, (((1,), (1,)), ((), ())), preferred_element_type=F32)


def layer_norm(x, gain):
    center = jnp.mean(x, axis=-1, keepdims=True)
    d = x - center
    spread = jnp.mean(d * d, axis=-1, keepdims=True)
    return (d * lax.rsqrt(spread + 1e-05) * gain).astype(BF)


def by_head(block):
    lane = lax.broadcasted_iota(jnp.int32, block.shape, 1) // 64
    empty = jnp.zeros((128 - SLOTS, 256), BF)
    parts = []
    for h in range(4):
        parts += [jnp.where(lane == h, block, jnp.zeros_like(block)), empty]
    return jnp.concatenate(parts, axis=0)


def attend(qkv, bases, masks):
    def scores(base):
        rows = pl.ds(base, SLOTS)
        k = qkv[rows, D : 2 * D]
        stacks = []
        for g in range(2):
            q = qkv[rows, g * 256 : g * 256 + 256]
            lane = lax.broadcasted_iota(jnp.int32, q.shape, 1) // 64
            stacks.append(jnp.concatenate([jnp.where(lane == h, q, jnp.zeros_like(q)) for h in range(4)], axis=0))
        low, high = k[:, 0:256], k[:, 256:512]
        return jnp.concatenate(
            [
                dot_t(low, stacks[0][0:256]),
                dot_t(low, jnp.concatenate([stacks[0][256:320], jnp.zeros((192, 256), BF)], axis=0))
                + dot_t(high, jnp.concatenate([jnp.zeros((64, 256), BF), stacks[1][0:192]], axis=0)),
                dot_t(high, stacks[1][192:320]),
            ],
            axis=1,
        )[0:72]

    def softmax(s, mask):
        if mask is not None:
            s = jnp.where(mask, s, -1e30)
        top = jnp.max(s, axis=0, keepdims=True)
        expo = jnp.exp2((s - top) * (0.125 * LOG2E))
        total = jnp.sum(expo, axis=0, keepdims=True)
        probs = expo * (1.0 / total)
        padded = jnp.concatenate([probs, jnp.zeros((56, 8 * SLOTS), F32)], axis=0)
        return padded.astype(BF).T

    def mix(probs, base):
        mixed = []
        for g in range(2):
            at = 2 * D + g * 256
            v = by_head(qkv[pl.ds(base, SLOTS), at : at + 256])
            wide = jnp.concatenate([probs[(4 * g + h) * SLOTS : (4 * g + h + 1) * SLOTS] for h in range(4)], axis=1)
            mixed.append(dot(wide, v).astype(BF))
        return jnp.concatenate(mixed, axis=1)

    count = len(bases)
    mixed, s, probs = [], scores(bases[0]), None
    for n in range(count):
        following = scores(bases[n + 1]) if n + 1 < count else None
        if probs is not None:
            mixed.append(mix(probs, bases[n - 1]))
        probs = softmax(s, masks[n])
        s = following
    mixed.append(mix(probs, bases[-1]))
    return mixed


def spread_out(result, slabs, chunk, base):
    parts = result.reshape(2, 4, 8, 256)
    lane = lax.broadcasted_iota(jnp.int32, (16, 128), 1)
    left = lane < 64
    even = (lane // 32) % 2 == 0
    for t in range(2):
        a = [parts[:, v, :, t * 128 : t * 128 + 128].reshape(16, 128) for v in range(4)]
        b0 = jnp.where(left, a[0], pltpu.roll(a[2], 64, 1))
        b1 = jnp.where(left, a[1], pltpu.roll(a[3], 64, 1))
        b2 = jnp.where(left, pltpu.roll(a[0], 64, 1), a[2])
        b3 = jnp.where(left, pltpu.roll(a[1], 64, 1), a[3])
        slabs[chunk, base + 4 * t] = jnp.where(even, b0, pltpu.roll(b1, 32, 1)).astype(BF)
        slabs[chunk, base + 4 * t + 1] = jnp.where(even, pltpu.roll(b0, 96, 1), b1).astype(BF)
        slabs[chunk, base + 4 * t + 2] = jnp.where(even, b2, pltpu.roll(b3, 32, 1)).astype(BF)
        slabs[chunk, base + 4 * t + 3] = jnp.where(even, pltpu.roll(b2, 96, 1), b3).astype(BF)


def kernel(n_lon, n_lat, *refs):
    (
        tok_h, first_h, gain1_h, wq1_h, wo1_h, second_h, gain2_h, wq2_h, wo2_h,
        high_h, north_h, low_h, gainm_h, wm_h, circle_h,
        out,
        tok, first, gain1, wq1, wo1, second, gain2, wq2, wo2,
        high, north, low, gainm, wm, circle,
        padded, x1, qkv, ones, east, x2, twos, above, slabs, inbox,
        load_sem, west_s, west_r, lat_s, lat_r, box_s, box_r,
    ) = refs
    lon = lax.axis_index("lon")
    lat = lax.axis_index("lat")
    west = lax.rem(lon + n_lon - 1, n_lon)
    owners = n_lon // 4
    up = lax.rem(lat + n_lat - 1, n_lat)
    down = lax.rem(lat + 1, n_lat)
    eastward = lax.rem(lon + 1, n_lon)

    sources = (tok_h, first_h, gain1_h, wq1_h, wo1_h, second_h, gain2_h, wq2_h, wo2_h,
               high_h, north_h, low_h, gainm_h, wm_h, circle_h)
    places = (tok, first, gain1, wq1, wo1, second, gain2, wq2, wo2,
              high, north, low, gainm, wm, circle)
    loads = [pltpu.make_async_copy(s, p, load_sem.at[n]) for n, (s, p) in enumerate(zip(sources, places))]
    (l_tok, l_first, l_gain1, l_wq1, l_wo1, l_second, l_gain2, l_wq2, l_wo2,
     l_high, l_north, l_low, l_gainm, l_wm, l_circle) = loads
    for load in (l_tok, l_first, l_gain1, l_wq1):
        load.start()

    barrier = pltpu.get_barrier_semaphore()

    def greet(t, carry):
        pl.semaphore_signal(
            barrier, inc=1, device_id={"lon": lax.rem(lon + t, n_lon), "lat": lat}, device_id_type=MESH
        )
        return carry

    lax.fori_loop(1, n_lon, greet, 0)
    for there in ((lon, up), (west, up), (lon, down), (eastward, down)):
        pl.semaphore_signal(
            barrier, inc=1, device_id={"lon": there[0], "lat": there[1]}, device_id_type=MESH
        )

    ones[WINDOWS, 0:WEST, :] = jnp.zeros((WEST, D), BF)
    east[WINDOWS, 32:WEST, :] = jnp.zeros((WEST - 32, D), BF)
    padded[:, 16:32, :] = jnp.zeros((12, 16, D), BF)

    @pl.when(lat == n_lat - 1)
    def _():
        ones[WINDOWS, WEST:SLOTS, :] = jnp.zeros((SLOTS - WEST, D), BF)
        east[WINDOWS, 0:32, :] = jnp.zeros((32, D), BF)


    l_tok.wait()
    padded[:, 0:30, :] = tok[...]
    def first_project(order):
        picks = jnp.concatenate([first[w * SLOTS : (w + 1) * SLOTS] for w in order], axis=0)
        x = dot(picks, padded[...].reshape(12 * 32, D))
        normed = layer_norm(x, gain1[...])
        for n, w in enumerate(order):
            x1[w * SLOTS : (w + 1) * SLOTS, :] = x[n * SLOTS : (n + 1) * SLOTS]
        return normed

    def first_heads(order, normed):
        for part in range(3):
            y = dot(normed, wq1[:, part * D : part * D + D]).astype(BF)
            for n, w in enumerate(order):
                qkv[w * SLOTS : (w + 1) * SLOTS, part * D : part * D + D] = y[n * SLOTS : (n + 1) * SLOTS]

    def first_block(order):
        mixed = attend(qkv, [w * SLOTS for w in order], [None] * len(order))
        update = dot(jnp.concatenate(mixed, axis=0), wo1[...])
        for n, w in enumerate(order):
            block = x1[w * SLOTS : (w + 1) * SLOTS, :] + update[n * SLOTS : (n + 1) * SLOTS]
            ones[w] = block.astype(BF)

    def remote(source, target, send, recv, there):
        return pltpu.make_async_remote_copy(
            src_ref=source,
            dst_ref=target,
            send_sem=send,
            recv_sem=recv,
            device_id={"lon": there[0], "lat": there[1]},
            device_id_type=MESH,
        )

    key = lax.broadcasted_iota(jnp.int32, (72, 8 * SLOTS), 0)
    query = lax.broadcasted_iota(jnp.int32, (72, 8 * SLOTS), 1) % SLOTS
    halo = {
        w: remote(ones.at[w, pl.ds(0, WEST)], east.at[w], west_s.at[w], west_r.at[w], (west, lat))
        for w in range(WINDOWS)
    }
    north_own = remote(
        ones.at[0, pl.ds(48, 32)], ones.at[WINDOWS, pl.ds(48, 32)], lat_s.at[0], lat_r.at[0], (lon, up)
    )
    north_west = remote(
        ones.at[0, pl.ds(0, 32)], east.at[WINDOWS, pl.ds(0, 32)], lat_s.at[1], lat_r.at[1], (west, up)
    )
    back = remote(twos.at[4, pl.ds(32, 48)], above, lat_s.at[2], lat_r.at[2], (lon, down))

    l_first.wait()
    l_gain1.wait()
    normed = first_project((0, 4))
    l_wq1.wait()
    for load in (l_wo1, l_second, l_gain2, l_wq2, l_wo2, l_wm, l_high, l_gainm, l_north, l_low, l_circle):
        load.start()
    first_heads((0, 4), normed)
    l_wo1.wait()
    first_block((0, 4))
    pl.semaphore_wait(barrier, n_lon - 1 + 4)

    @pl.when(lat != 0)
    def _():
        north_own.start()
        north_west.start()

    halo[4].start()
    halo[0].start()
    first_heads((3, 2, 1), first_project((3, 2, 1)))
    first_block((3, 2))
    halo[3].start()
    halo[2].start()
    first_block((1,))
    halo[1].start()
    l_second.wait()
    l_gain2.wait()
    l_wq2.wait()
    l_wo2.wait()
    def gather(w):
        x2[w * SLOTS : (w + 1) * SLOTS, :] = dot(
            second[:, 0 : 2 * SLOTS], ones[w : w + 2].reshape(2 * SLOTS, D)
        ) + dot(second[:, 2 * SLOTS :], east[w : w + 2].reshape(2 * WEST, D))

    def project(first_w, last_w):
        span = slice(first_w * SLOTS, (last_w + 1) * SLOTS)
        normed = layer_norm(x2[span, :], gain2[...])
        for n in range(3):
            qkv[span, n * D : n * D + D] = dot(normed, wq2[:, n * D : n * D + D]).astype(BF)

    def finish(order, masks):
        mixed = attend(qkv, [w * SLOTS for w in order], masks)
        update = dot(jnp.concatenate(mixed, axis=0), wo2[...])
        for n, w in enumerate(order):
            block = x2[w * SLOTS : (w + 1) * SLOTS, :] + update[n * SLOTS : (n + 1) * SLOTS]
            twos[w] = block.astype(BF)

    def merge(quads, chunk, aside_jobs=()):
        aside_jobs = list(aside_jobs)
        quads = quads.reshape(4, 64, D)
        center = jnp.sum(jnp.sum(quads, axis=0), axis=-1, keepdims=True) / (4 * D)
        apart = quads - center[None]
        spread = jnp.sum(jnp.sum(apart * apart, axis=0), axis=-1, keepdims=True) / (4 * D)
        scaled = apart * lax.rsqrt(spread + 1e-05)[None]
        normed = [(scaled[q] * gainm[:, q * D : q * D + D]).astype(BF) for q in range(4)]
        normed = jnp.concatenate(normed, axis=1)
        def post(result, quarter, skip):
            spread_out(result, slabs, chunk, quarter * owners)
            for turn in range(skip, owners):
                beside = lon - lon // owners * owners + turn
                there = quarter * owners + jnp.where(beside >= owners, beside - owners, beside)
                remote(
                    slabs.at[chunk, there], inbox.at[chunk, lon], box_s.at[chunk], box_r.at[chunk], (there, lat)
                ).start()

        made = None
        for aside, beyond in ((1, 1), (0, 1), (1, 0), (0, 0)):
            quarter = lax.rem(lon // (2 * owners) + aside, 2) * 2 + lax.rem(lon // owners + beyond, 2)
            columns = pl.ds(pl.multiple_of(quarter * (owners * FEATS), owners * FEATS), owners * FEATS)
            result = dot(normed, wm[:, columns])
            if aside_jobs:
                aside_jobs.pop(0)()
            if made is not None:
                post(*made, 0)
            made = (result, quarter)
        post(*made, 1)
        inbox[chunk, lon] = slabs[chunk, lon]

    def parcels(chunk):
        return remote(
            slabs.at[chunk, pl.ds(0, n_lon - 1)], inbox.at[chunk, pl.ds(0, n_lon - 1)], box_s.at[chunk], box_r.at[chunk],
            (west, lat),
        )

    parted = ((key < 36) == (query < 36)) | (lat != n_lat - 1)
    halo[4].wait_recv()
    halo[0].wait_recv()

    @pl.when(lat == 0)
    def _():
        span = slice(4 * SLOTS, 5 * SLOTS)
        x2[span, :] = dot(second[:, SLOTS : 2 * SLOTS], ones[0]) + dot(second[:, 2 * SLOTS + WEST :], east[0])
        project(4, 4)
        mixed = attend(qkv, [4 * SLOTS], [(key < 36) == (query < 36)])
        block = x2[span, :] + dot(mixed[0], wo2[...])
        above[...] = block[32:SLOTS].astype(BF)

    @pl.when(lat != n_lat - 1)
    def _():
        north_own.wait_recv()
        north_west.wait_recv()

    gather(4)
    project(4, 4)
    finish((4,), [parted])

    @pl.when(lat != n_lat - 1)
    def _():
        back.start()

    halo[3].wait_recv()
    halo[2].wait_recv()
    gather(3)
    gather(2)
    project(2, 3)
    finish((3, 2), [None, None])
    l_high.wait()
    l_gainm.wait()
    l_wm.wait()
    halo[1].wait_recv()
    kept = []

    def early():
        gather(1)
        gather(0)

    def middle():
        kept.append(layer_norm(x2[0 : 2 * SLOTS, :], gain2[...]))
        qkv[0 : 2 * SLOTS, 0:D] = dot(kept[0], wq2[:, 0:D]).astype(BF)

    def keys():
        qkv[0 : 2 * SLOTS, D : 2 * D] = dot(kept[0], wq2[:, D : 2 * D]).astype(BF)

    def values():
        qkv[0 : 2 * SLOTS, 2 * D :] = dot(kept[0], wq2[:, 2 * D :]).astype(BF)

    merge(dot(high[...], twos[2:5].reshape(3 * SLOTS, D)), 1, (early, middle, keys, values))
    finish((1, 0), [None, None])

    @pl.when(lat != 0)
    def _():
        back.wait_recv()

    l_north.wait()
    l_low.wait()
    merge(dot(north[...], above[...]) + dot(low[...], twos[0:3].reshape(3 * SLOTS, D)), 0)

    l_circle.wait()
    for chunk in (1, 0):
        parcels(chunk).wait_recv()
        held = inbox[chunk].reshape(n_lon * 16, 128)
        laid = lax.dot_general(held, circle[...], (((0,), (0,)), ((), ())), preferred_element_type=F32)
        laid = laid.astype(BF)
        for i in range(8 if chunk == 0 else 7):
            half, v = divmod(i, 4)
            out[chunk * 8 + i] = laid[v * FEATS : (v + 1) * FEATS, half * 256 : half * 256 + 192]

    for w in range(WINDOWS):
        halo[w].wait_send()

    @pl.when(lat != 0)
    def _():
        north_own.wait_send()
        north_west.wait_send()

    @pl.when(lat != n_lat - 1)
    def _():
        back.wait_send()


    for chunk in range(2):
        parcels(chunk).wait_send()


def solution(mesh):
    n_lon, n_lat = mesh.shape["lon"], mesh.shape["lat"]

    def local(tokens, gain_one, w_qkv_one, w_out_one, gain_two, w_qkv_two, w_out_two, merge_gain, w_merge):
        first, second, high, north, low, circle = tables(n_lon)
        operands = (
            jnp.swapaxes(tokens, 0, 1), first, gain_one.reshape(1, D), w_qkv_one, w_out_one, second,
            gain_two.reshape(1, D), w_qkv_two, w_out_two, high, north, low,
            merge_gain.reshape(1, 4 * D), w_merge, circle,
        )
        out = pl.pallas_call(
            functools.partial(kernel, n_lon, n_lat),
            out_shape=pltpu.VMEM((15, FEATS, 6 * n_lon), BF),
            in_specs=[pl.BlockSpec(memory_space=pltpu.HBM)] * len(operands),
            out_specs=pl.BlockSpec(memory_space=pltpu.VMEM),
            scratch_shapes=[pltpu.VMEM(o.shape, o.dtype) for o in operands]
            + [
                pltpu.VMEM((12, 32, D), BF),
                pltpu.VMEM((WINDOWS * SLOTS, D), F32),
                pltpu.VMEM((WINDOWS * SLOTS, 3 * D), BF),
                pltpu.VMEM((WINDOWS + 1, SLOTS, D), BF),
                pltpu.VMEM((WINDOWS + 1, WEST, D), BF),
                pltpu.VMEM((WINDOWS * SLOTS, D), F32),
                pltpu.VMEM((WINDOWS, SLOTS, D), BF),
                pltpu.VMEM((WEST, D), BF),
                pltpu.VMEM((2, n_lon, 16, 128), BF),
                pltpu.VMEM((2, n_lon, 16, 128), BF),
                pltpu.SemaphoreType.DMA((len(operands),)),
                pltpu.SemaphoreType.DMA((WINDOWS,)),
                pltpu.SemaphoreType.DMA((WINDOWS,)),
                pltpu.SemaphoreType.DMA((3,)),
                pltpu.SemaphoreType.DMA((3,)),
                pltpu.SemaphoreType.DMA((2,)),
                pltpu.SemaphoreType.DMA((2,)),
            ],
            compiler_params=pltpu.CompilerParams(
                collective_id=0, has_side_effects=True, vmem_limit_bytes=56 * 1024 * 1024
            ),
        )(*operands)
        return jnp.swapaxes(out, 1, 2)[None]

    return jax.shard_map(
        local,
        mesh=mesh,
        in_specs=(P("lat", "lon", None), P(), P(), P(), P(), P(), P(), P(), P()),
        out_specs=P("lat", None, None, "lon"),
        check_vma=False,
    )
```

```python
import functools

import jax
import jax.numpy as jnp
import numpy as np
from jax import lax
from jax.experimental import pallas as pl
from jax.experimental.pallas import tpu as pltpu
from jax.sharding import PartitionSpec as P

MESH = pl.DeviceIdType.MESH
BF = jnp.bfloat16
F32 = jnp.float32

D = 512
SLOTS = 80
WINDOWS = 5
LOG2E = 1.4426950408889634
WEST = 48
FEATS = 32


def tables(n_lon):
    first = np.zeros((WINDOWS * SLOTS, 12 * 32), np.float32)
    for w in range(WINDOWS):
        for r in range(6):
            for c in range(12):
                if c < 6:
                    slot = (0 if r < 3 else 18) + (r % 3) * 6 + c
                else:
                    slot = (54 if r < 3 else 36) + (r % 3) * 6 + c - 6
                first[w * SLOTS + slot, c * 32 + 6 * w + r] = 1
    second = np.zeros((SLOTS, 2 * SLOTS + 2 * WEST), np.float32)
    for r in range(6):
        for c in range(12):
            within = (r % 3) * 6 + c % 6
            if c < 6:
                source = 36 + within if r < 3 else SLOTS + 54 + within
            else:
                source = 2 * SLOTS + (18 + within if r < 3 else WEST + within)
            second[r * 12 + c, source] = 1
    high = np.zeros((256, 3 * SLOTS), np.float32)
    low = np.zeros((256, WEST + 3 * SLOTS), np.float32)
    for corner in range(4):
        for i in range(15):
            for j in range(6):
                row = 2 * i + corner % 2
                col = 2 * j + corner // 2
                spot = corner * 64 + (i % 8) * 8 + j
                if row < 3:
                    low[spot, 4 + row * 12 + col] = 1
                    continue
                w, r = divmod(row - 3, 6)
                if i >= 8:
                    high[spot, (w - 2) * SLOTS + r * 12 + col] = 1
                else:
                    low[spot, WEST + w * SLOTS + r * 12 + col] = 1
    circle = np.zeros((n_lon * 16, 512), np.float32)
    for s in range(n_lon):
        for half in range(2):
            for j in range(6):
                circle[s * 16 + half * 8 + j, half * 256 + (6 * s + 3 + j) % (6 * n_lon)] = 1
    return [jnp.asarray(t, BF) for t in (first, second, high, low, circle)]


def dot(a, b):
    return jnp.dot(a, b, preferred_element_type=F32)


def dot_t(a, b):
    return lax.dot_general(a, b, (((1,), (1,)), ((), ())), preferred_element_type=F32)


def layer_norm(x, gain):
    center = jnp.mean(x, axis=-1, keepdims=True)
    d = x - center
    spread = jnp.mean(d * d, axis=-1, keepdims=True)
    return (d * lax.rsqrt(spread + 1e-05) * gain).astype(BF)


def by_head(block):
    lane = lax.broadcasted_iota(jnp.int32, block.shape, 1) // 64
    empty = jnp.zeros((128 - SLOTS, 256), BF)
    parts = []
    for h in range(4):
        parts += [jnp.where(lane == h, block, jnp.zeros_like(block)), empty]
    return jnp.concatenate(parts, axis=0)


def attend(qkv, bases, masks, jobs=()):
    def scores(base):
        rows = pl.ds(base, SLOTS)
        k = qkv[rows, D : 2 * D]
        stacks = []
        for g in range(2):
            q = qkv[rows, g * 256 : g * 256 + 256]
            lane = lax.broadcasted_iota(jnp.int32, q.shape, 1) // 64
            stacks.append(jnp.concatenate([jnp.where(lane == h, q, jnp.zeros_like(q)) for h in range(4)], axis=0))
        low, high = k[:, 0:256], k[:, 256:512]
        return jnp.concatenate(
            [
                dot_t(low, stacks[0][0:256]),
                dot_t(low, jnp.concatenate([stacks[0][256:320], jnp.zeros((192, 256), BF)], axis=0))
                + dot_t(high, jnp.concatenate([jnp.zeros((64, 256), BF), stacks[1][0:192]], axis=0)),
                dot_t(high, stacks[1][192:320]),
            ],
            axis=1,
        )[0:72]

    def softmax(s, mask):
        if mask is not None:
            s = jnp.where(mask, s, -1e30)
        top = jnp.max(s, axis=0, keepdims=True)
        expo = jnp.exp2((s - top) * (0.125 * LOG2E))
        total = jnp.sum(expo, axis=0, keepdims=True)
        probs = expo * (1.0 / total)
        padded = jnp.concatenate([probs, jnp.zeros((56, 8 * SLOTS), F32)], axis=0)
        return padded.astype(BF).T

    def mix(probs, base):
        mixed = []
        for g in range(2):
            at = 2 * D + g * 256
            v = by_head(qkv[pl.ds(base, SLOTS), at : at + 256])
            wide = jnp.concatenate([probs[(4 * g + h) * SLOTS : (4 * g + h + 1) * SLOTS] for h in range(4)], axis=1)
            mixed.append(dot(wide, v).astype(BF))
        return jnp.concatenate(mixed, axis=1)

    count = len(bases)
    jobs = list(jobs)
    mixed, s, probs = [], scores(bases[0]), None
    for n in range(count):
        following = scores(bases[n + 1]) if n + 1 < count else None
        if probs is not None:
            mixed.append(mix(probs, bases[n - 1]))
        probs = softmax(s, masks[n])
        if jobs:
            jobs.pop(0)()
        s = following
    mixed.append(mix(probs, bases[-1]))
    return mixed


def spread_out(result, slabs, chunk, base):
    parts = result.reshape(2, 4, 8, 256)
    lane = lax.broadcasted_iota(jnp.int32, (16, 128), 1)
    left = lane < 64
    even = (lane // 32) % 2 == 0
    for t in range(2):
        a = [parts[:, v, :, t * 128 : t * 128 + 128].reshape(16, 128) for v in range(4)]
        b0 = jnp.where(left, a[0], pltpu.roll(a[2], 64, 1))
        b1 = jnp.where(left, a[1], pltpu.roll(a[3], 64, 1))
        b2 = jnp.where(left, pltpu.roll(a[0], 64, 1), a[2])
        b3 = jnp.where(left, pltpu.roll(a[1], 64, 1), a[3])
        slabs[chunk, base + 4 * t] = jnp.where(even, b0, pltpu.roll(b1, 32, 1)).astype(BF)
        slabs[chunk, base + 4 * t + 1] = jnp.where(even, pltpu.roll(b0, 96, 1), b1).astype(BF)
        slabs[chunk, base + 4 * t + 2] = jnp.where(even, b2, pltpu.roll(b3, 32, 1)).astype(BF)
        slabs[chunk, base + 4 * t + 3] = jnp.where(even, pltpu.roll(b2, 96, 1), b3).astype(BF)


def kernel(n_lon, n_lat, *refs):
    (
        tok_h, first_h, gain1_h, wq1_h, wo1_h, second_h, gain2_h, wq2_h, wo2_h,
        high_h, low_h, gainm_h, wm_h, circle_h,
        out,
        tok, first, gain1, wq1, wo1, second, gain2, wq2, wo2,
        high, low, gainm, wm, circle,
        padded, x1, qkv, ones, east, x2, twos, above, slabs, inbox,
        load_sem, west_s, west_r, lat_s, lat_r, box_s, box_r,
    ) = refs
    lon = lax.axis_index("lon")
    lat = lax.axis_index("lat")
    west = lax.rem(lon + n_lon - 1, n_lon)
    owners = n_lon // 4
    up = lax.rem(lat + n_lat - 1, n_lat)
    down = lax.rem(lat + 1, n_lat)
    eastward = lax.rem(lon + 1, n_lon)

    sources = (tok_h, first_h, gain1_h, wq1_h, wo1_h, second_h, gain2_h, wq2_h, wo2_h,
               high_h, low_h, gainm_h, wm_h, circle_h)
    places = (tok, first, gain1, wq1, wo1, second, gain2, wq2, wo2,
              high, low, gainm, wm, circle)
    loads = [pltpu.make_async_copy(s, p, load_sem.at[n]) for n, (s, p) in enumerate(zip(sources, places))]
    (l_tok, l_first, l_gain1, l_wq1, l_wo1, l_second, l_gain2, l_wq2, l_wo2,
     l_high, l_low, l_gainm, l_wm, l_circle) = loads
    for load in (l_tok, l_first, l_gain1, l_wq1):
        load.start()

    barrier = pltpu.get_barrier_semaphore()

    def greet(t, carry):
        pl.semaphore_signal(
            barrier, inc=1, device_id={"lon": lax.rem(lon + t, n_lon), "lat": lat}, device_id_type=MESH
        )
        return carry

    lax.fori_loop(1, n_lon, greet, 0)
    for there in ((lon, up), (west, up), (lon, down), (eastward, down)):
        pl.semaphore_signal(
            barrier, inc=1, device_id={"lon": there[0], "lat": there[1]}, device_id_type=MESH
        )

    ones[WINDOWS, 0:WEST, :] = jnp.zeros((WEST, D), BF)
    east[WINDOWS, 32:WEST, :] = jnp.zeros((WEST - 32, D), BF)
    padded[:, 16:32, :] = jnp.zeros((12, 16, D), BF)

    @pl.when(lat == n_lat - 1)
    def _():
        ones[WINDOWS, WEST:SLOTS, :] = jnp.zeros((SLOTS - WEST, D), BF)
        east[WINDOWS, 0:32, :] = jnp.zeros((32, D), BF)


    l_tok.wait()
    padded[:, 0:30, :] = tok[...]
    def first_project(order):
        picks = jnp.concatenate([first[w * SLOTS : (w + 1) * SLOTS] for w in order], axis=0)
        x = dot(picks, padded[...].reshape(12 * 32, D))
        normed = layer_norm(x, gain1[...])
        for n, w in enumerate(order):
            x1[w * SLOTS : (w + 1) * SLOTS, :] = x[n * SLOTS : (n + 1) * SLOTS]
        return normed

    def first_heads(order, normed):
        for part in range(3):
            y = dot(normed, wq1[:, part * D : part * D + D]).astype(BF)
            for n, w in enumerate(order):
                qkv[w * SLOTS : (w + 1) * SLOTS, part * D : part * D + D] = y[n * SLOTS : (n + 1) * SLOTS]

    def first_block(order):
        mixed = attend(qkv, [w * SLOTS for w in order], [None] * len(order))
        update = dot(jnp.concatenate(mixed, axis=0), wo1[...])
        for n, w in enumerate(order):
            block = x1[w * SLOTS : (w + 1) * SLOTS, :] + update[n * SLOTS : (n + 1) * SLOTS]
            ones[w] = block.astype(BF)

    def remote(source, target, send, recv, there):
        return pltpu.make_async_remote_copy(
            src_ref=source,
            dst_ref=target,
            send_sem=send,
            recv_sem=recv,
            device_id={"lon": there[0], "lat": there[1]},
            device_id_type=MESH,
        )

    key = lax.broadcasted_iota(jnp.int32, (72, 8 * SLOTS), 0)
    query = lax.broadcasted_iota(jnp.int32, (72, 8 * SLOTS), 1) % SLOTS
    halo = {
        w: remote(ones.at[w, pl.ds(0, WEST)], east.at[w], west_s.at[w], west_r.at[w], (west, lat))
        for w in range(WINDOWS)
    }
    north_own = remote(
        ones.at[0, pl.ds(48, 32)], ones.at[WINDOWS, pl.ds(48, 32)], lat_s.at[0], lat_r.at[0], (lon, up)
    )
    north_west = remote(
        ones.at[0, pl.ds(0, 32)], east.at[WINDOWS, pl.ds(0, 32)], lat_s.at[1], lat_r.at[1], (west, up)
    )
    back = remote(twos.at[4, pl.ds(32, 48)], above, lat_s.at[2], lat_r.at[2], (lon, down))

    l_first.wait()
    l_gain1.wait()
    normed = first_project((0, 4))
    l_wq1.wait()
    for load in (l_wo1, l_second, l_gain2, l_wq2, l_wo2, l_wm, l_high, l_gainm, l_low, l_circle):
        load.start()
    first_heads((0, 4), normed)
    l_wo1.wait()
    first_block((0, 4))
    pl.semaphore_wait(barrier, n_lon - 1 + 4)

    @pl.when(lat != 0)
    def _():
        north_own.start()
        north_west.start()

    halo[4].start()
    halo[0].start()
    first_heads((3, 2, 1), first_project((3, 2, 1)))
    first_block((3, 2, 1))
    halo[3].start()
    halo[2].start()
    halo[1].start()
    l_second.wait()
    l_gain2.wait()
    l_wq2.wait()
    l_wo2.wait()
    def gather(w):
        tokens = [ones[w : w + 2].reshape(2 * SLOTS, D), east[w : w + 2].reshape(2 * WEST, D)]
        x2[w * SLOTS : (w + 1) * SLOTS, :] = dot(second[...], jnp.concatenate(tokens, axis=0))

    def project(first_w, last_w):
        span = slice(first_w * SLOTS, (last_w + 1) * SLOTS)
        normed = layer_norm(x2[span, :], gain2[...])
        for n in range(3):
            qkv[span, n * D : n * D + D] = dot(normed, wq2[:, n * D : n * D + D]).astype(BF)

    def finish(order, masks, jobs=()):
        mixed = attend(qkv, [w * SLOTS for w in order], masks, jobs)
        update = dot(jnp.concatenate(mixed, axis=0), wo2[...])
        for n, w in enumerate(order):
            block = x2[w * SLOTS : (w + 1) * SLOTS, :] + update[n * SLOTS : (n + 1) * SLOTS]
            twos[w] = block.astype(BF)

    def merge(quads, chunk, aside_jobs=()):
        aside_jobs = list(aside_jobs)
        quads = quads.reshape(4, 64, D)
        center = jnp.sum(jnp.sum(quads, axis=0), axis=-1, keepdims=True) / (4 * D)
        apart = quads - center[None]
        spread = jnp.sum(jnp.sum(apart * apart, axis=0), axis=-1, keepdims=True) / (4 * D)
        scaled = apart * lax.rsqrt(spread + 1e-05)[None]
        normed = [(scaled[q] * gainm[:, q * D : q * D + D]).astype(BF) for q in range(4)]
        normed = jnp.concatenate(normed, axis=1)
        def post(result, quarter, skip):
            spread_out(result, slabs, chunk, quarter * owners)
            for turn in range(skip, owners):
                beside = lon - lon // owners * owners + turn
                there = quarter * owners + jnp.where(beside >= owners, beside - owners, beside)
                remote(
                    slabs.at[chunk, there], inbox.at[chunk, lon], box_s.at[chunk], box_r.at[chunk], (there, lat)
                ).start()

        made = None
        for aside, beyond in ((1, 1), (0, 1), (1, 0), (0, 0)):
            quarter = lax.rem(lon // (2 * owners) + aside, 2) * 2 + lax.rem(lon // owners + beyond, 2)
            columns = pl.ds(pl.multiple_of(quarter * (owners * FEATS), owners * FEATS), owners * FEATS)
            result = dot(normed, wm[:, columns])
            if aside_jobs:
                aside_jobs.pop(0)()
            if made is not None:
                post(*made, 0)
            made = (result, quarter)
        post(*made, 1)
        inbox[chunk, lon] = slabs[chunk, lon]

    def parcels(chunk):
        return remote(
            slabs.at[chunk, pl.ds(0, n_lon - 1)], inbox.at[chunk, pl.ds(0, n_lon - 1)], box_s.at[chunk], box_r.at[chunk],
            (west, lat),
        )

    parted = ((key < 36) == (query < 36)) | (lat != n_lat - 1)
    halo[4].wait_recv()
    halo[0].wait_recv()

    @pl.when(lat == 0)
    def _():
        span = slice(4 * SLOTS, 5 * SLOTS)
        x2[span, :] = dot(second[:, SLOTS : 2 * SLOTS], ones[0]) + dot(second[:, 2 * SLOTS + WEST :], east[0])
        project(4, 4)
        mixed = attend(qkv, [4 * SLOTS], [(key < 36) == (query < 36)])
        block = x2[span, :] + dot(mixed[0], wo2[...])
        above[...] = block[32:SLOTS].astype(BF)

    @pl.when(lat != n_lat - 1)
    def _():
        north_own.wait_recv()
        north_west.wait_recv()

    def jobs_of(low, high):
        span = slice(low * SLOTS, (high + 1) * SLOTS)
        kept = []

        def gathers():
            for w in range(high, low - 1, -1):
                gather(w)

        def queries():
            kept.append(layer_norm(x2[span, :], gain2[...]))
            qkv[span, 0:D] = dot(kept[0], wq2[:, 0:D]).astype(BF)

        def keys():
            qkv[span, D : 2 * D] = dot(kept[0], wq2[:, D : 2 * D]).astype(BF)

        def values():
            qkv[span, 2 * D :] = dot(kept[0], wq2[:, 2 * D :]).astype(BF)

        return gathers, queries, keys, values

    gather(4)
    project(4, 4)
    halo[3].wait_recv()
    halo[2].wait_recv()
    gathers, queries, keys, values = jobs_of(2, 3)

    def both():
        gathers()
        queries()

    finish((4,), [parted], (both,))

    @pl.when(lat != n_lat - 1)
    def _():
        back.start()

    keys()
    values()
    finish((3, 2), [None, None])
    l_high.wait()
    l_gainm.wait()
    l_wm.wait()
    halo[1].wait_recv()
    merge(dot(high[...], twos[2:5].reshape(3 * SLOTS, D)), 1, jobs_of(0, 1))
    finish((1, 0), [None, None])

    @pl.when(lat != 0)
    def _():
        back.wait_recv()

    l_low.wait()
    picks = jnp.concatenate([above[...], twos[0:3].reshape(3 * SLOTS, D)], axis=0)
    merge(dot(low[...], picks), 0)

    l_circle.wait()
    for chunk in (1, 0):
        parcels(chunk).wait_recv()
        held = inbox[chunk].reshape(n_lon * 16, 128)
        laid = lax.dot_general(held, circle[...], (((0,), (0,)), ((), ())), preferred_element_type=F32)
        laid = laid.astype(BF)
        for i in range(8 if chunk == 0 else 7):
            half, v = divmod(i, 4)
            out[chunk * 8 + i] = laid[v * FEATS : (v + 1) * FEATS, half * 256 : half * 256 + 192]

    for w in range(WINDOWS):
        halo[w].wait_send()

    @pl.when(lat != 0)
    def _():
        north_own.wait_send()
        north_west.wait_send()

    @pl.when(lat != n_lat - 1)
    def _():
        back.wait_send()


    for chunk in range(2):
        parcels(chunk).wait_send()


def solution(mesh):
    n_lon, n_lat = mesh.shape["lon"], mesh.shape["lat"]

    def local(tokens, gain_one, w_qkv_one, w_out_one, gain_two, w_qkv_two, w_out_two, merge_gain, w_merge):
        first, second, high, low, circle = tables(n_lon)
        operands = (
            jnp.swapaxes(tokens, 0, 1), first, gain_one.reshape(1, D), w_qkv_one, w_out_one, second,
            gain_two.reshape(1, D), w_qkv_two, w_out_two, high, low,
            merge_gain.reshape(1, 4 * D), w_merge, circle,
        )
        out = pl.pallas_call(
            functools.partial(kernel, n_lon, n_lat),
            out_shape=pltpu.VMEM((15, FEATS, 6 * n_lon), BF),
            in_specs=[pl.BlockSpec(memory_space=pltpu.HBM)] * len(operands),
            out_specs=pl.BlockSpec(memory_space=pltpu.VMEM),
            scratch_shapes=[pltpu.VMEM(o.shape, o.dtype) for o in operands]
            + [
                pltpu.VMEM((12, 32, D), BF),
                pltpu.VMEM((WINDOWS * SLOTS, D), F32),
                pltpu.VMEM((WINDOWS * SLOTS, 3 * D), BF),
                pltpu.VMEM((WINDOWS + 1, SLOTS, D), BF),
                pltpu.VMEM((WINDOWS + 1, WEST, D), BF),
                pltpu.VMEM((WINDOWS * SLOTS, D), F32),
                pltpu.VMEM((WINDOWS, SLOTS, D), BF),
                pltpu.VMEM((WEST, D), BF),
                pltpu.VMEM((2, n_lon, 16, 128), BF),
                pltpu.VMEM((2, n_lon, 16, 128), BF),
                pltpu.SemaphoreType.DMA((len(operands),)),
                pltpu.SemaphoreType.DMA((WINDOWS,)),
                pltpu.SemaphoreType.DMA((WINDOWS,)),
                pltpu.SemaphoreType.DMA((3,)),
                pltpu.SemaphoreType.DMA((3,)),
                pltpu.SemaphoreType.DMA((2,)),
                pltpu.SemaphoreType.DMA((2,)),
            ],
            compiler_params=pltpu.CompilerParams(
                collective_id=0, has_side_effects=True, vmem_limit_bytes=56 * 1024 * 1024
            ),
        )(*operands)
        return jnp.swapaxes(out, 1, 2)[None]

    return jax.shard_map(
        local,
        mesh=mesh,
        in_specs=(P("lat", "lon", None), P(), P(), P(), P(), P(), P(), P(), P()),
        out_specs=P("lat", None, None, "lon"),
        check_vma=False,
    )
```

```python
import functools

import jax
import jax.numpy as jnp
import numpy as np
from jax import lax
from jax.experimental import pallas as pl
from jax.experimental.pallas import tpu as pltpu
from jax.sharding import PartitionSpec as P

MESH = pl.DeviceIdType.MESH
BF = jnp.bfloat16
F32 = jnp.float32

D = 512
SLOTS = 80
WINDOWS = 5
LOG2E = 1.4426950408889634
WEST = 48
FEATS = 32


def tables(n_lon):
    first = np.zeros((WINDOWS * SLOTS, 12 * 32), np.float32)
    for w in range(WINDOWS):
        for r in range(6):
            for c in range(12):
                if c < 6:
                    slot = (0 if r < 3 else 18) + (r % 3) * 6 + c
                else:
                    slot = (54 if r < 3 else 36) + (r % 3) * 6 + c - 6
                first[w * SLOTS + slot, c * 32 + 6 * w + r] = 1
    second = np.zeros((SLOTS, 2 * SLOTS + 2 * WEST), np.float32)
    for r in range(6):
        for c in range(12):
            within = (r % 3) * 6 + c % 6
            if c < 6:
                source = 36 + within if r < 3 else SLOTS + 54 + within
            else:
                source = 2 * SLOTS + (18 + within if r < 3 else WEST + within)
            second[r * 12 + c, source] = 1
    high = np.zeros((256, 3 * SLOTS), np.float32)
    low = np.zeros((256, WEST + 3 * SLOTS), np.float32)
    for corner in range(4):
        for i in range(15):
            for j in range(6):
                row = 2 * i + corner % 2
                col = 2 * j + corner // 2
                spot = corner * 64 + (i % 8) * 8 + j
                if row < 3:
                    low[spot, 4 + row * 12 + col] = 1
                    continue
                w, r = divmod(row - 3, 6)
                if i >= 8:
                    high[spot, (w - 2) * SLOTS + r * 12 + col] = 1
                else:
                    low[spot, WEST + w * SLOTS + r * 12 + col] = 1
    circle = np.zeros((n_lon * 16, 512), np.float32)
    for s in range(n_lon):
        for half in range(2):
            for j in range(6):
                circle[s * 16 + half * 8 + j, half * 256 + (6 * s + 3 + j) % (6 * n_lon)] = 1
    return [jnp.asarray(t, BF) for t in (first, second, high, low, circle)]


def dot(a, b):
    return jnp.dot(a, b, preferred_element_type=F32)


def dot_t(a, b):
    return lax.dot_general(a, b, (((1,), (1,)), ((), ())), preferred_element_type=F32)


def layer_norm(x, gain):
    center = jnp.mean(x, axis=-1, keepdims=True)
    d = x - center
    spread = jnp.mean(d * d, axis=-1, keepdims=True)
    return (d * lax.rsqrt(spread + 1e-05) * gain).astype(BF)


def by_head(block):
    lane = lax.broadcasted_iota(jnp.int32, block.shape, 1) // 64
    empty = jnp.zeros((128 - SLOTS, 256), BF)
    parts = []
    for h in range(4):
        parts += [jnp.where(lane == h, block, jnp.zeros_like(block)), empty]
    return jnp.concatenate(parts, axis=0)


def attend(qkv, bases, masks, jobs=()):
    def scores(base):
        rows = pl.ds(base, SLOTS)
        k = qkv[rows, D : 2 * D]
        stacks = []
        for g in range(2):
            q = qkv[rows, g * 256 : g * 256 + 256]
            lane = lax.broadcasted_iota(jnp.int32, q.shape, 1) // 64
            stacks.append(jnp.concatenate([jnp.where(lane == h, q, jnp.zeros_like(q)) for h in range(4)], axis=0))
        low, high = k[:, 0:256], k[:, 256:512]
        return jnp.concatenate(
            [
                dot_t(low, stacks[0][0:256]),
                dot_t(low, jnp.concatenate([stacks[0][256:320], jnp.zeros((192, 256), BF)], axis=0))
                + dot_t(high, jnp.concatenate([jnp.zeros((64, 256), BF), stacks[1][0:192]], axis=0)),
                dot_t(high, stacks[1][192:320]),
            ],
            axis=1,
        )[0:72]

    def softmax(s, mask):
        if mask is not None:
            s = jnp.where(mask, s, -1e30)
        top = jnp.max(s, axis=0, keepdims=True)
        expo = jnp.exp2((s - top) * (0.125 * LOG2E))
        total = jnp.sum(expo, axis=0, keepdims=True)
        probs = expo * (1.0 / total)
        padded = jnp.concatenate([probs, jnp.zeros((56, 8 * SLOTS), F32)], axis=0)
        return padded.astype(BF).T

    def mix(probs, base):
        mixed = []
        for g in range(2):
            at = 2 * D + g * 256
            v = by_head(qkv[pl.ds(base, SLOTS), at : at + 256])
            wide = jnp.concatenate([probs[(4 * g + h) * SLOTS : (4 * g + h + 1) * SLOTS] for h in range(4)], axis=1)
            mixed.append(dot(wide, v).astype(BF))
        return jnp.concatenate(mixed, axis=1)

    count = len(bases)
    jobs = list(jobs)
    mixed, s, probs = [], scores(bases[0]), None
    for n in range(count):
        following = scores(bases[n + 1]) if n + 1 < count else None
        if probs is not None:
            mixed.append(mix(probs, bases[n - 1]))
        probs = softmax(s, masks[n])
        if jobs:
            jobs.pop(0)()
        s = following
    mixed.append(mix(probs, bases[-1]))
    return mixed


def spread_out(result, slabs, chunk, base):
    parts = result.reshape(2, 4, 8, 256)
    lane = lax.broadcasted_iota(jnp.int32, (16, 128), 1)
    left = lane < 64
    even = (lane // 32) % 2 == 0
    for t in range(2):
        a = [parts[:, v, :, t * 128 : t * 128 + 128].reshape(16, 128) for v in range(4)]
        b0 = jnp.where(left, a[0], pltpu.roll(a[2], 64, 1))
        b1 = jnp.where(left, a[1], pltpu.roll(a[3], 64, 1))
        b2 = jnp.where(left, pltpu.roll(a[0], 64, 1), a[2])
        b3 = jnp.where(left, pltpu.roll(a[1], 64, 1), a[3])
        slabs[chunk, base + 4 * t] = jnp.where(even, b0, pltpu.roll(b1, 32, 1)).astype(BF)
        slabs[chunk, base + 4 * t + 1] = jnp.where(even, pltpu.roll(b0, 96, 1), b1).astype(BF)
        slabs[chunk, base + 4 * t + 2] = jnp.where(even, b2, pltpu.roll(b3, 32, 1)).astype(BF)
        slabs[chunk, base + 4 * t + 3] = jnp.where(even, pltpu.roll(b2, 96, 1), b3).astype(BF)


def kernel(n_lon, n_lat, *refs):
    (
        tok_h, first_h, gain1_h, wq1_h, wo1_h, second_h, gain2_h, wq2_h, wo2_h,
        high_h, low_h, gainm_h, wm_h, circle_h,
        out,
        tok, first, gain1, wq1, wo1, second, gain2, wq2, wo2,
        high, low, gainm, wm, circle,
        padded, x1, qkv, ones, east, x2, twos, above, slabs, inbox,
        load_sem, west_s, west_r, lat_s, lat_r, box_s, box_r,
    ) = refs
    lon = lax.axis_index("lon")
    lat = lax.axis_index("lat")
    west = lax.rem(lon + n_lon - 1, n_lon)
    owners = n_lon // 4
    up = lax.rem(lat + n_lat - 1, n_lat)
    down = lax.rem(lat + 1, n_lat)
    eastward = lax.rem(lon + 1, n_lon)

    sources = (tok_h, first_h, gain1_h, wq1_h, wo1_h, second_h, gain2_h, wq2_h, wo2_h,
               high_h, low_h, gainm_h, wm_h, circle_h)
    places = (tok, first, gain1, wq1, wo1, second, gain2, wq2, wo2,
              high, low, gainm, wm, circle)
    loads = [pltpu.make_async_copy(s, p, load_sem.at[n]) for n, (s, p) in enumerate(zip(sources, places))]
    (l_tok, l_first, l_gain1, l_wq1, l_wo1, l_second, l_gain2, l_wq2, l_wo2,
     l_high, l_low, l_gainm, l_wm, l_circle) = loads
    for load in (l_tok, l_first, l_gain1, l_wq1):
        load.start()

    barrier = pltpu.get_barrier_semaphore()

    def greet(t, carry):
        pl.semaphore_signal(
            barrier, inc=1, device_id={"lon": lax.rem(lon + t, n_lon), "lat": lat}, device_id_type=MESH
        )
        return carry

    lax.fori_loop(1, n_lon, greet, 0)
    for there in ((lon, up), (west, up), (lon, down), (eastward, down)):
        pl.semaphore_signal(
            barrier, inc=1, device_id={"lon": there[0], "lat": there[1]}, device_id_type=MESH
        )

    ones[WINDOWS, 0:WEST, :] = jnp.zeros((WEST, D), BF)
    east[WINDOWS, 32:WEST, :] = jnp.zeros((WEST - 32, D), BF)
    padded[:, 16:32, :] = jnp.zeros((12, 16, D), BF)

    @pl.when(lat == n_lat - 1)
    def _():
        ones[WINDOWS, WEST:SLOTS, :] = jnp.zeros((SLOTS - WEST, D), BF)
        east[WINDOWS, 0:32, :] = jnp.zeros((32, D), BF)


    l_tok.wait()
    padded[:, 0:30, :] = tok[...]
    def first_project(order):
        picks = jnp.concatenate([first[w * SLOTS : (w + 1) * SLOTS] for w in order], axis=0)
        x = dot(picks, padded[...].reshape(12 * 32, D))
        normed = layer_norm(x, gain1[...])
        for n, w in enumerate(order):
            x1[w * SLOTS : (w + 1) * SLOTS, :] = x[n * SLOTS : (n + 1) * SLOTS]
        return normed

    def first_heads(order, normed):
        for part in range(3):
            y = dot(normed, wq1[:, part * D : part * D + D]).astype(BF)
            for n, w in enumerate(order):
                qkv[w * SLOTS : (w + 1) * SLOTS, part * D : part * D + D] = y[n * SLOTS : (n + 1) * SLOTS]

    def first_block(order):
        mixed = attend(qkv, [w * SLOTS for w in order], [None] * len(order))
        update = dot(jnp.concatenate(mixed, axis=0), wo1[...])
        for n, w in enumerate(order):
            block = x1[w * SLOTS : (w + 1) * SLOTS, :] + update[n * SLOTS : (n + 1) * SLOTS]
            ones[w] = block.astype(BF)

    def remote(source, target, send, recv, there):
        return pltpu.make_async_remote_copy(
            src_ref=source,
            dst_ref=target,
            send_sem=send,
            recv_sem=recv,
            device_id={"lon": there[0], "lat": there[1]},
            device_id_type=MESH,
        )

    key = lax.broadcasted_iota(jnp.int32, (72, 8 * SLOTS), 0)
    query = lax.broadcasted_iota(jnp.int32, (72, 8 * SLOTS), 1) % SLOTS
    halo = {
        w: remote(ones.at[w, pl.ds(0, WEST)], east.at[w], west_s.at[w], west_r.at[w], (west, lat))
        for w in range(WINDOWS)
    }
    north_own = remote(
        ones.at[0, pl.ds(48, 32)], ones.at[WINDOWS, pl.ds(48, 32)], lat_s.at[0], lat_r.at[0], (lon, up)
    )
    north_west = remote(
        ones.at[0, pl.ds(0, 32)], east.at[WINDOWS, pl.ds(0, 32)], lat_s.at[1], lat_r.at[1], (west, up)
    )
    back = remote(twos.at[4, pl.ds(32, 48)], above, lat_s.at[2], lat_r.at[2], (lon, down))

    l_first.wait()
    l_gain1.wait()
    normed = first_project((0, 4))
    l_wq1.wait()
    for load in (l_wo1, l_second, l_gain2, l_wq2, l_wo2, l_wm, l_high, l_gainm, l_low, l_circle):
        load.start()
    first_heads((0, 4), normed)
    l_wo1.wait()
    first_block((0, 4))
    pl.semaphore_wait(barrier, n_lon - 1 + 4)

    @pl.when(lat != 0)
    def _():
        north_own.start()
        north_west.start()

    halo[4].start()
    halo[0].start()
    first_heads((3, 2, 1), first_project((3, 2, 1)))
    first_block((3, 2, 1))
    halo[3].start()
    halo[2].start()
    halo[1].start()
    l_second.wait()
    l_gain2.wait()
    l_wq2.wait()
    l_wo2.wait()
    def gather(w):
        tokens = [ones[w : w + 2].reshape(2 * SLOTS, D), east[w : w + 2].reshape(2 * WEST, D)]
        x2[w * SLOTS : (w + 1) * SLOTS, :] = dot(second[...], jnp.concatenate(tokens, axis=0))

    def project(first_w, last_w):
        span = slice(first_w * SLOTS, (last_w + 1) * SLOTS)
        normed = layer_norm(x2[span, :], gain2[...])
        for n in range(3):
            qkv[span, n * D : n * D + D] = dot(normed, wq2[:, n * D : n * D + D]).astype(BF)

    def finish(order, masks, jobs=()):
        mixed = attend(qkv, [w * SLOTS for w in order], masks, jobs)
        update = dot(jnp.concatenate(mixed, axis=0), wo2[...])
        for n, w in enumerate(order):
            block = x2[w * SLOTS : (w + 1) * SLOTS, :] + update[n * SLOTS : (n + 1) * SLOTS]
            twos[w] = block.astype(BF)

    def merge(quads, chunk, aside_jobs=()):
        aside_jobs = list(aside_jobs)
        quads = quads.reshape(4, 64, D)
        center = jnp.sum(jnp.sum(quads, axis=0), axis=-1, keepdims=True) / (4 * D)
        apart = quads - center[None]
        spread = jnp.sum(jnp.sum(apart * apart, axis=0), axis=-1, keepdims=True) / (4 * D)
        scaled = apart * lax.rsqrt(spread + 1e-05)[None]
        normed = [(scaled[q] * gainm[:, q * D : q * D + D]).astype(BF) for q in range(4)]
        normed = jnp.concatenate(normed, axis=1)
        def post(result, quarter, skip):
            spread_out(result, slabs, chunk, quarter * owners)
            for turn in range(skip, owners):
                beside = lon - lon // owners * owners + turn
                there = quarter * owners + jnp.where(beside >= owners, beside - owners, beside)
                remote(
                    slabs.at[chunk, there], inbox.at[chunk, lon], box_s.at[chunk], box_r.at[chunk, lon // owners], (there, lat)
                ).start()

        made = None
        for aside, beyond in ((1, 1), (0, 1), (1, 0), (0, 0)):
            quarter = lax.rem(lon // (2 * owners) + aside, 2) * 2 + lax.rem(lon // owners + beyond, 2)
            columns = pl.ds(pl.multiple_of(quarter * (owners * FEATS), owners * FEATS), owners * FEATS)
            result = dot(normed, wm[:, columns])
            if aside_jobs:
                aside_jobs.pop(0)()
            if made is not None:
                post(*made, 0)
            made = (result, quarter)
        post(*made, 1)
        inbox[chunk, lon] = slabs[chunk, lon]

    def parcels(chunk, quarter, count):
        return remote(
            slabs.at[chunk, pl.ds(0, count)], inbox.at[chunk, pl.ds(0, count)], box_s.at[chunk],
            box_r.at[chunk, quarter], (west, lat),
        )

    parted = ((key < 36) == (query < 36)) | (lat != n_lat - 1)
    halo[4].wait_recv()
    halo[0].wait_recv()

    @pl.when(lat == 0)
    def _():
        span = slice(4 * SLOTS, 5 * SLOTS)
        x2[span, :] = dot(second[:, SLOTS : 2 * SLOTS], ones[0]) + dot(second[:, 2 * SLOTS + WEST :], east[0])
        project(4, 4)
        mixed = attend(qkv, [4 * SLOTS], [(key < 36) == (query < 36)])
        block = x2[span, :] + dot(mixed[0], wo2[...])
        above[...] = block[32:SLOTS].astype(BF)

    @pl.when(lat != n_lat - 1)
    def _():
        north_own.wait_recv()
        north_west.wait_recv()

    def jobs_of(low, high):
        span = slice(low * SLOTS, (high + 1) * SLOTS)
        kept = []

        def gathers():
            for w in range(high, low - 1, -1):
                gather(w)

        def queries():
            kept.append(layer_norm(x2[span, :], gain2[...]))
            qkv[span, 0:D] = dot(kept[0], wq2[:, 0:D]).astype(BF)

        def keys():
            qkv[span, D : 2 * D] = dot(kept[0], wq2[:, D : 2 * D]).astype(BF)

        def values():
            qkv[span, 2 * D :] = dot(kept[0], wq2[:, 2 * D :]).astype(BF)

        return gathers, queries, keys, values

    gather(4)
    project(4, 4)
    halo[3].wait_recv()
    halo[2].wait_recv()
    gathers, queries, keys, values = jobs_of(2, 3)

    def both():
        gathers()
        queries()

    finish((4,), [parted], (both,))

    @pl.when(lat != n_lat - 1)
    def _():
        back.start()

    keys()
    values()
    finish((3, 2), [None, None])
    l_high.wait()
    l_gainm.wait()
    l_wm.wait()
    halo[1].wait_recv()
    merge(dot(high[...], twos[2:5].reshape(3 * SLOTS, D)), 1, jobs_of(0, 1))
    finish((1, 0), [None, None])

    @pl.when(lat != 0)
    def _():
        back.wait_recv()

    l_low.wait()
    picks = jnp.concatenate([above[...], twos[0:3].reshape(3 * SLOTS, D)], axis=0)
    merge(dot(low[...], picks), 0)

    l_circle.wait()
    for chunk in (1, 0):
        laid = None
        for aside, beyond in ((0, 0), (1, 0), (0, 1), (1, 1)):
            quarter = lax.rem(lon // (2 * owners) + aside, 2) * 2 + lax.rem(lon // owners + beyond, 2)
            parcels(chunk, quarter, owners if aside + beyond else owners - 1).wait_recv()
            held = inbox[chunk, pl.ds(quarter * owners, owners)].reshape(owners * 16, 128)
            places = circle[pl.ds(pl.multiple_of(quarter * (owners * 16), owners * 16), owners * 16), :]
            part = lax.dot_general(held, places, (((0,), (0,)), ((), ())), preferred_element_type=F32)
            laid = part if laid is None else laid + part
        laid = laid.astype(BF)
        for i in range(8 if chunk == 0 else 7):
            half, v = divmod(i, 4)
            out[chunk * 8 + i] = laid[v * FEATS : (v + 1) * FEATS, half * 256 : half * 256 + 192]

    for w in range(WINDOWS):
        halo[w].wait_send()

    @pl.when(lat != 0)
    def _():
        north_own.wait_send()
        north_west.wait_send()

    @pl.when(lat != n_lat - 1)
    def _():
        back.wait_send()


    for chunk in range(2):
        parcels(chunk, 0, n_lon - 1).wait_send()


def solution(mesh):
    n_lon, n_lat = mesh.shape["lon"], mesh.shape["lat"]

    def local(tokens, gain_one, w_qkv_one, w_out_one, gain_two, w_qkv_two, w_out_two, merge_gain, w_merge):
        first, second, high, low, circle = tables(n_lon)
        operands = (
            jnp.swapaxes(tokens, 0, 1), first, gain_one.reshape(1, D), w_qkv_one, w_out_one, second,
            gain_two.reshape(1, D), w_qkv_two, w_out_two, high, low,
            merge_gain.reshape(1, 4 * D), w_merge, circle,
        )
        out = pl.pallas_call(
            functools.partial(kernel, n_lon, n_lat),
            out_shape=pltpu.VMEM((15, FEATS, 6 * n_lon), BF),
            in_specs=[pl.BlockSpec(memory_space=pltpu.HBM)] * len(operands),
            out_specs=pl.BlockSpec(memory_space=pltpu.VMEM),
            scratch_shapes=[pltpu.VMEM(o.shape, o.dtype) for o in operands]
            + [
                pltpu.VMEM((12, 32, D), BF),
                pltpu.VMEM((WINDOWS * SLOTS, D), F32),
                pltpu.VMEM((WINDOWS * SLOTS, 3 * D), BF),
                pltpu.VMEM((WINDOWS + 1, SLOTS, D), BF),
                pltpu.VMEM((WINDOWS + 1, WEST, D), BF),
                pltpu.VMEM((WINDOWS * SLOTS, D), F32),
                pltpu.VMEM((WINDOWS, SLOTS, D), BF),
                pltpu.VMEM((WEST, D), BF),
                pltpu.VMEM((2, n_lon, 16, 128), BF),
                pltpu.VMEM((2, n_lon, 16, 128), BF),
                pltpu.SemaphoreType.DMA((len(operands),)),
                pltpu.SemaphoreType.DMA((WINDOWS,)),
                pltpu.SemaphoreType.DMA((WINDOWS,)),
                pltpu.SemaphoreType.DMA((3,)),
                pltpu.SemaphoreType.DMA((3,)),
                pltpu.SemaphoreType.DMA((2,)),
                pltpu.SemaphoreType.DMA((2, 4)),
            ],
            compiler_params=pltpu.CompilerParams(
                collective_id=0, has_side_effects=True, vmem_limit_bytes=56 * 1024 * 1024
            ),
        )(*operands)
        return jnp.swapaxes(out, 1, 2)[None]

    return jax.shard_map(
        local,
        mesh=mesh,
        in_specs=(P("lat", "lon", None), P(), P(), P(), P(), P(), P(), P(), P()),
        out_specs=P("lat", None, None, "lon"),
        check_vma=False,
    )
```

```python
import functools

import jax
import jax.numpy as jnp
import numpy as np
from jax import lax
from jax.experimental import pallas as pl
from jax.experimental.pallas import tpu as pltpu
from jax.sharding import PartitionSpec as P

MESH = pl.DeviceIdType.MESH
BF = jnp.bfloat16
F32 = jnp.float32

D = 512
SLOTS = 80
WINDOWS = 5
LOG2E = 1.4426950408889634
WEST = 48
FEATS = 32


def tables(n_lon):
    first = np.zeros((WINDOWS * SLOTS, 12 * 32), np.float32)
    for w in range(WINDOWS):
        for r in range(6):
            for c in range(12):
                if c < 6:
                    slot = (0 if r < 3 else 18) + (r % 3) * 6 + c
                else:
                    slot = (54 if r < 3 else 36) + (r % 3) * 6 + c - 6
                first[w * SLOTS + slot, c * 32 + 6 * w + r] = 1
    second = np.zeros((SLOTS, 2 * SLOTS + 2 * WEST), np.float32)
    for r in range(6):
        for c in range(12):
            within = (r % 3) * 6 + c % 6
            if c < 6:
                source = 36 + within if r < 3 else SLOTS + 54 + within
            else:
                source = 2 * SLOTS + (18 + within if r < 3 else WEST + within)
            second[r * 12 + c, source] = 1
    high = np.zeros((256, 3 * SLOTS), np.float32)
    low = np.zeros((256, WEST + 3 * SLOTS), np.float32)
    for corner in range(4):
        for i in range(15):
            for j in range(6):
                row = 2 * i + corner % 2
                col = 2 * j + corner // 2
                spot = corner * 64 + (i % 8) * 8 + j
                if row < 3:
                    low[spot, 4 + row * 12 + col] = 1
                    continue
                w, r = divmod(row - 3, 6)
                if i >= 8:
                    high[spot, (w - 2) * SLOTS + r * 12 + col] = 1
                else:
                    low[spot, WEST + w * SLOTS + r * 12 + col] = 1
    circle = np.zeros((n_lon * 16, 512), np.float32)
    for s in range(n_lon):
        for half in range(2):
            for j in range(6):
                circle[s * 16 + half * 8 + j, half * 256 + (6 * s + 3 + j) % (6 * n_lon)] = 1
    return [jnp.asarray(t, BF) for t in (first, second, high, low, circle)]


def dot(a, b):
    return jnp.dot(a, b, preferred_element_type=F32)


def dot_t(a, b):
    return lax.dot_general(a, b, (((1,), (1,)), ((), ())), preferred_element_type=F32)


def layer_norm(x, gain):
    center = jnp.mean(x, axis=-1, keepdims=True)
    d = x - center
    spread = jnp.mean(d * d, axis=-1, keepdims=True)
    return (d * lax.rsqrt(spread + 1e-05) * gain).astype(BF)


def by_head(block):
    lane = lax.broadcasted_iota(jnp.int32, block.shape, 1) // 64
    empty = jnp.zeros((128 - SLOTS, 256), BF)
    parts = []
    for h in range(4):
        parts += [jnp.where(lane == h, block, jnp.zeros_like(block)), empty]
    return jnp.concatenate(parts, axis=0)


def attend(qkv, bases, masks, jobs=()):
    def scores(base):
        rows = pl.ds(base, SLOTS)
        k = qkv[rows, D : 2 * D]
        stacks = []
        for g in range(2):
            q = qkv[rows, g * 256 : g * 256 + 256]
            lane = lax.broadcasted_iota(jnp.int32, q.shape, 1) // 64
            stacks.append(jnp.concatenate([jnp.where(lane == h, q, jnp.zeros_like(q)) for h in range(4)], axis=0))
        low, high = k[:, 0:256], k[:, 256:512]
        return jnp.concatenate(
            [
                dot_t(low, stacks[0][0:256]),
                dot_t(low, jnp.concatenate([stacks[0][256:320], jnp.zeros((192, 256), BF)], axis=0))
                + dot_t(high, jnp.concatenate([jnp.zeros((64, 256), BF), stacks[1][0:192]], axis=0)),
                dot_t(high, stacks[1][192:320]),
            ],
            axis=1,
        )[0:72]

    def softmax(s, mask):
        if mask is not None:
            s = jnp.where(mask, s, -1e30)
        top = jnp.max(s, axis=0, keepdims=True)
        expo = jnp.exp2((s - top) * (0.125 * LOG2E))
        total = jnp.sum(expo, axis=0, keepdims=True)
        probs = expo * (1.0 / total)
        padded = jnp.concatenate([probs, jnp.zeros((56, 8 * SLOTS), F32)], axis=0)
        return padded.astype(BF).T

    def mix(probs, base):
        mixed = []
        for g in range(2):
            at = 2 * D + g * 256
            v = by_head(qkv[pl.ds(base, SLOTS), at : at + 256])
            wide = jnp.concatenate([probs[(4 * g + h) * SLOTS : (4 * g + h + 1) * SLOTS] for h in range(4)], axis=1)
            mixed.append(dot(wide, v).astype(BF))
        return jnp.concatenate(mixed, axis=1)

    count = len(bases)
    jobs = list(jobs)
    mixed, s, probs = [], scores(bases[0]), None
    for n in range(count):
        following = scores(bases[n + 1]) if n + 1 < count else None
        if probs is not None:
            mixed.append(mix(probs, bases[n - 1]))
        probs = softmax(s, masks[n])
        if jobs:
            jobs.pop(0)()
        s = following
    mixed.append(mix(probs, bases[-1]))
    return mixed


def spread_out(result, slabs, chunk, base):
    parts = result.reshape(2, 4, 8, 256)
    lane = lax.broadcasted_iota(jnp.int32, (16, 128), 1)
    left = lane < 64
    even = (lane // 32) % 2 == 0
    for t in range(2):
        a = [parts[:, v, :, t * 128 : t * 128 + 128].reshape(16, 128) for v in range(4)]
        b0 = jnp.where(left, a[0], pltpu.roll(a[2], 64, 1))
        b1 = jnp.where(left, a[1], pltpu.roll(a[3], 64, 1))
        b2 = jnp.where(left, pltpu.roll(a[0], 64, 1), a[2])
        b3 = jnp.where(left, pltpu.roll(a[1], 64, 1), a[3])
        slabs[chunk, base + 4 * t] = jnp.where(even, b0, pltpu.roll(b1, 32, 1)).astype(BF)
        slabs[chunk, base + 4 * t + 1] = jnp.where(even, pltpu.roll(b0, 96, 1), b1).astype(BF)
        slabs[chunk, base + 4 * t + 2] = jnp.where(even, b2, pltpu.roll(b3, 32, 1)).astype(BF)
        slabs[chunk, base + 4 * t + 3] = jnp.where(even, pltpu.roll(b2, 96, 1), b3).astype(BF)


def kernel(n_lon, n_lat, *refs):
    (
        tok_h, first_h, gain1_h, wq1_h, wo1_h, second_h, gain2_h, wq2_h, wo2_h,
        high_h, low_h, gainm_h, wm_h, circle_h,
        out,
        tok, first, gain1, wq1, wo1, second, gain2, wq2, wo2,
        high, low, gainm, wm, circle,
        padded, x1, qkv, ones, east, x2, twos, above, slabs, inbox,
        load_sem, west_s, west_r, lat_s, lat_r, box_s, box_r,
    ) = refs
    lon = lax.axis_index("lon")
    lat = lax.axis_index("lat")
    west = lax.rem(lon + n_lon - 1, n_lon)
    owners = n_lon // 4
    up = lax.rem(lat + n_lat - 1, n_lat)
    down = lax.rem(lat + 1, n_lat)
    eastward = lax.rem(lon + 1, n_lon)

    sources = (tok_h, first_h, gain1_h, wq1_h, wo1_h, second_h, gain2_h, wq2_h, wo2_h,
               high_h, low_h, gainm_h, wm_h, circle_h)
    places = (tok, first, gain1, wq1, wo1, second, gain2, wq2, wo2,
              high, low, gainm, wm, circle)
    loads = [pltpu.make_async_copy(s, p, load_sem.at[n]) for n, (s, p) in enumerate(zip(sources, places))]
    (l_tok, l_first, l_gain1, l_wq1, l_wo1, l_second, l_gain2, l_wq2, l_wo2,
     l_high, l_low, l_gainm, l_wm, l_circle) = loads
    for load in (l_tok, l_first, l_gain1, l_wq1):
        load.start()

    barrier = pltpu.get_barrier_semaphore()

    def greet(t, carry):
        pl.semaphore_signal(
            barrier, inc=1, device_id={"lon": lax.rem(lon + t, n_lon), "lat": lat}, device_id_type=MESH
        )
        return carry

    lax.fori_loop(1, n_lon, greet, 0)
    for there in ((lon, up), (west, up), (lon, down), (eastward, down)):
        pl.semaphore_signal(
            barrier, inc=1, device_id={"lon": there[0], "lat": there[1]}, device_id_type=MESH
        )

    ones[WINDOWS, 0:WEST, :] = jnp.zeros((WEST, D), BF)
    east[WINDOWS, 32:WEST, :] = jnp.zeros((WEST - 32, D), BF)
    padded[:, 16:32, :] = jnp.zeros((12, 16, D), BF)

    @pl.when(lat == n_lat - 1)
    def _():
        ones[WINDOWS, WEST:SLOTS, :] = jnp.zeros((SLOTS - WEST, D), BF)
        east[WINDOWS, 0:32, :] = jnp.zeros((32, D), BF)


    l_tok.wait()
    padded[:, 0:30, :] = tok[...]
    def first_project(order):
        picks = jnp.concatenate([first[w * SLOTS : (w + 1) * SLOTS] for w in order], axis=0)
        x = dot(picks, padded[...].reshape(12 * 32, D))
        normed = layer_norm(x, gain1[...])
        for n, w in enumerate(order):
            x1[w * SLOTS : (w + 1) * SLOTS, :] = x[n * SLOTS : (n + 1) * SLOTS]
        return normed

    def first_heads(order, normed):
        for part in range(3):
            y = dot(normed, wq1[:, part * D : part * D + D]).astype(BF)
            for n, w in enumerate(order):
                qkv[w * SLOTS : (w + 1) * SLOTS, part * D : part * D + D] = y[n * SLOTS : (n + 1) * SLOTS]

    def first_block(order):
        mixed = attend(qkv, [w * SLOTS for w in order], [None] * len(order))
        update = dot(jnp.concatenate(mixed, axis=0), wo1[...])
        for n, w in enumerate(order):
            block = x1[w * SLOTS : (w + 1) * SLOTS, :] + update[n * SLOTS : (n + 1) * SLOTS]
            ones[w] = block.astype(BF)

    def remote(source, target, send, recv, there):
        return pltpu.make_async_remote_copy(
            src_ref=source,
            dst_ref=target,
            send_sem=send,
            recv_sem=recv,
            device_id={"lon": there[0], "lat": there[1]},
            device_id_type=MESH,
        )

    key = lax.broadcasted_iota(jnp.int32, (72, 8 * SLOTS), 0)
    query = lax.broadcasted_iota(jnp.int32, (72, 8 * SLOTS), 1) % SLOTS
    halo = {
        w: remote(ones.at[w, pl.ds(0, WEST)], east.at[w], west_s.at[w], west_r.at[w], (west, lat))
        for w in range(WINDOWS)
    }
    north_own = remote(
        ones.at[0, pl.ds(48, 32)], ones.at[WINDOWS, pl.ds(48, 32)], lat_s.at[0], lat_r.at[0], (lon, up)
    )
    north_west = remote(
        ones.at[0, pl.ds(0, 32)], east.at[WINDOWS, pl.ds(0, 32)], lat_s.at[1], lat_r.at[1], (west, up)
    )
    back = remote(twos.at[4, pl.ds(32, 48)], above, lat_s.at[2], lat_r.at[2], (lon, down))

    l_first.wait()
    l_gain1.wait()
    normed = first_project((0, 4))
    l_wq1.wait()
    for load in (l_wo1, l_second, l_gain2, l_wq2, l_wo2, l_wm, l_high, l_gainm, l_low, l_circle):
        load.start()
    first_heads((0, 4), normed)
    l_wo1.wait()
    first_block((0, 4))
    pl.semaphore_wait(barrier, n_lon - 1 + 4)

    @pl.when(lat != 0)
    def _():
        north_own.start()
        north_west.start()

    halo[4].start()
    halo[0].start()
    first_heads((3, 2, 1), first_project((3, 2, 1)))
    first_block((3, 2, 1))
    halo[3].start()
    halo[2].start()
    halo[1].start()
    l_second.wait()
    l_gain2.wait()
    l_wq2.wait()
    l_wo2.wait()
    def gather(w):
        tokens = [ones[w : w + 2].reshape(2 * SLOTS, D), east[w : w + 2].reshape(2 * WEST, D)]
        x2[w * SLOTS : (w + 1) * SLOTS, :] = dot(second[...], jnp.concatenate(tokens, axis=0))

    def project(first_w, last_w):
        span = slice(first_w * SLOTS, (last_w + 1) * SLOTS)
        normed = layer_norm(x2[span, :], gain2[...])
        for n in range(3):
            qkv[span, n * D : n * D + D] = dot(normed, wq2[:, n * D : n * D + D]).astype(BF)

    def finish(order, masks, jobs=()):
        mixed = attend(qkv, [w * SLOTS for w in order], masks, jobs)
        update = dot(jnp.concatenate(mixed, axis=0), wo2[...])
        for n, w in enumerate(order):
            block = x2[w * SLOTS : (w + 1) * SLOTS, :] + update[n * SLOTS : (n + 1) * SLOTS]
            twos[w] = block.astype(BF)

    def merge(quads, chunk, aside_jobs=()):
        aside_jobs = list(aside_jobs)
        quads = quads.reshape(4, 64, D)
        center = jnp.sum(jnp.sum(quads, axis=0), axis=-1, keepdims=True) / (4 * D)
        apart = quads - center[None]
        spread = jnp.sum(jnp.sum(apart * apart, axis=0), axis=-1, keepdims=True) / (4 * D)
        scaled = apart * lax.rsqrt(spread + 1e-05)[None]
        normed = [(scaled[q] * gainm[:, q * D : q * D + D]).astype(BF) for q in range(4)]
        normed = jnp.concatenate(normed, axis=1)
        def post(result, quarter, skip):
            spread_out(result, slabs, chunk, quarter * owners)
            for turn in range(skip, owners):
                beside = lon - lon // owners * owners + turn
                there = quarter * owners + jnp.where(beside >= owners, beside - owners, beside)
                remote(
                    slabs.at[chunk, there], inbox.at[chunk, lon], box_s.at[chunk], box_r.at[chunk], (there, lat)
                ).start()

        made = None
        for aside, beyond in ((0, 1), (1, 1), (0, 0), (1, 0)):
            quarter = lax.rem(lon // (2 * owners) + aside, 2) * 2 + lax.rem(lon // owners + beyond, 2)
            columns = pl.ds(pl.multiple_of(quarter * (owners * FEATS), owners * FEATS), owners * FEATS)
            result = dot(normed, wm[:, columns])
            if aside_jobs:
                aside_jobs.pop(0)()
            if made is not None:
                post(*made)
            made = (result, quarter, 0 if aside + beyond else 1)
        post(*made)
        inbox[chunk, lon] = slabs[chunk, lon]

    def parcels(chunk):
        return remote(
            slabs.at[chunk, pl.ds(0, n_lon - 1)], inbox.at[chunk, pl.ds(0, n_lon - 1)], box_s.at[chunk], box_r.at[chunk],
            (west, lat),
        )

    parted = ((key < 36) == (query < 36)) | (lat != n_lat - 1)
    halo[4].wait_recv()
    halo[0].wait_recv()

    @pl.when(lat == 0)
    def _():
        span = slice(4 * SLOTS, 5 * SLOTS)
        x2[span, :] = dot(second[:, SLOTS : 2 * SLOTS], ones[0]) + dot(second[:, 2 * SLOTS + WEST :], east[0])
        project(4, 4)
        mixed = attend(qkv, [4 * SLOTS], [(key < 36) == (query < 36)])
        block = x2[span, :] + dot(mixed[0], wo2[...])
        above[...] = block[32:SLOTS].astype(BF)

    @pl.when(lat != n_lat - 1)
    def _():
        north_own.wait_recv()
        north_west.wait_recv()

    def jobs_of(low, high):
        span = slice(low * SLOTS, (high + 1) * SLOTS)
        kept = []

        def gathers():
            for w in range(high, low - 1, -1):
                gather(w)

        def queries():
            kept.append(layer_norm(x2[span, :], gain2[...]))
            qkv[span, 0:D] = dot(kept[0], wq2[:, 0:D]).astype(BF)

        def keys():
            qkv[span, D : 2 * D] = dot(kept[0], wq2[:, D : 2 * D]).astype(BF)

        def values():
            qkv[span, 2 * D :] = dot(kept[0], wq2[:, 2 * D :]).astype(BF)

        return gathers, queries, keys, values

    gather(4)
    project(4, 4)
    halo[3].wait_recv()
    halo[2].wait_recv()
    gathers, queries, keys, values = jobs_of(2, 3)

    def both():
        gathers()
        queries()

    finish((4,), [parted], (both,))

    @pl.when(lat != n_lat - 1)
    def _():
        back.start()

    keys()
    values()
    finish((3, 2), [None, None])
    l_high.wait()
    l_gainm.wait()
    l_wm.wait()
    halo[1].wait_recv()
    merge(dot(high[...], twos[2:5].reshape(3 * SLOTS, D)), 1, jobs_of(0, 1))
    finish((1, 0), [None, None])

    @pl.when(lat != 0)
    def _():
        back.wait_recv()

    l_low.wait()
    picks = jnp.concatenate([above[...], twos[0:3].reshape(3 * SLOTS, D)], axis=0)
    merge(dot(low[...], picks), 0)

    l_circle.wait()
    for chunk in (1, 0):
        parcels(chunk).wait_recv()
        held = inbox[chunk].reshape(n_lon * 16, 128)
        laid = lax.dot_general(held, circle[...], (((0,), (0,)), ((), ())), preferred_element_type=F32)
        laid = laid.astype(BF)
        for i in range(8 if chunk == 0 else 7):
            half, v = divmod(i, 4)
            out[chunk * 8 + i] = laid[v * FEATS : (v + 1) * FEATS, half * 256 : half * 256 + 192]

    for w in range(WINDOWS):
        halo[w].wait_send()

    @pl.when(lat != 0)
    def _():
        north_own.wait_send()
        north_west.wait_send()

    @pl.when(lat != n_lat - 1)
    def _():
        back.wait_send()


    for chunk in range(2):
        parcels(chunk).wait_send()


def solution(mesh):
    n_lon, n_lat = mesh.shape["lon"], mesh.shape["lat"]

    def local(tokens, gain_one, w_qkv_one, w_out_one, gain_two, w_qkv_two, w_out_two, merge_gain, w_merge):
        first, second, high, low, circle = tables(n_lon)
        operands = (
            jnp.swapaxes(tokens, 0, 1), first, gain_one.reshape(1, D), w_qkv_one, w_out_one, second,
            gain_two.reshape(1, D), w_qkv_two, w_out_two, high, low,
            merge_gain.reshape(1, 4 * D), w_merge, circle,
        )
        out = pl.pallas_call(
            functools.partial(kernel, n_lon, n_lat),
            out_shape=pltpu.VMEM((15, FEATS, 6 * n_lon), BF),
            in_specs=[pl.BlockSpec(memory_space=pltpu.HBM)] * len(operands),
            out_specs=pl.BlockSpec(memory_space=pltpu.VMEM),
            scratch_shapes=[pltpu.VMEM(o.shape, o.dtype) for o in operands]
            + [
                pltpu.VMEM((12, 32, D), BF),
                pltpu.VMEM((WINDOWS * SLOTS, D), F32),
                pltpu.VMEM((WINDOWS * SLOTS, 3 * D), BF),
                pltpu.VMEM((WINDOWS + 1, SLOTS, D), BF),
                pltpu.VMEM((WINDOWS + 1, WEST, D), BF),
                pltpu.VMEM((WINDOWS * SLOTS, D), F32),
                pltpu.VMEM((WINDOWS, SLOTS, D), BF),
                pltpu.VMEM((WEST, D), BF),
                pltpu.VMEM((2, n_lon, 16, 128), BF),
                pltpu.VMEM((2, n_lon, 16, 128), BF),
                pltpu.SemaphoreType.DMA((len(operands),)),
                pltpu.SemaphoreType.DMA((WINDOWS,)),
                pltpu.SemaphoreType.DMA((WINDOWS,)),
                pltpu.SemaphoreType.DMA((3,)),
                pltpu.SemaphoreType.DMA((3,)),
                pltpu.SemaphoreType.DMA((2,)),
                pltpu.SemaphoreType.DMA((2,)),
            ],
            compiler_params=pltpu.CompilerParams(
                collective_id=0, has_side_effects=True, vmem_limit_bytes=56 * 1024 * 1024
            ),
        )(*operands)
        return jnp.swapaxes(out, 1, 2)[None]

    return jax.shard_map(
        local,
        mesh=mesh,
        in_specs=(P("lat", "lon", None), P(), P(), P(), P(), P(), P(), P(), P()),
        out_specs=P("lat", None, None, "lon"),
        check_vma=False,
    )
```
